256 devices in a mesh: tm: 32 (over z, x), tmpl: 8 (over y, core).
Axes of the slice: x: 4, y: 4, z: 8, core: 2. Of those that a mesh axis runs over, the one named last changes fastest.
Arguments:
- strain: float32 [2, 3, 4194304], P(None, None, 'tm'), may hold values from -6 to 6
- templates: float32 [2, 8, 2048, 2048], P(None, 'tmpl', 'tm'), may hold values from -6 to 6
- pattern: int32 [8, 1024], P('tmpl'), may hold values 0 or 1
- cutoff: int32 [8], P('tmpl'), may hold values from 256 to 1024
Outputs:
- snr_power: float32 [8, 4194304], P('tmpl', 'tm')
- bank_peak: float32 [4194304], P('tm')
The draws below stay inside these ranges and needn't reach their ends.
All inputs are finite; a program needn't handle non-finite values. No bound on the sum of `pattern` on one device may be relied on, other than what follows from the above.
Results may differ from the reference program's by a relative error of at most 0.000092.
Values sent between devices are 32-bit elements; how exact they have to be, the bound alone decides.
No kernel may reach another device: no remote copies, remote signals or barrier semaphores. Data moves between devices by JAX's collectives and lax.ppermute only.
A program may use at most 128 MiB of HBM per device.

```python
import jax
import jax.numpy as jnp
from jax import lax

SPLIT = 2048
NLEN = 4194304
DET = 3
BD = 2
NFB = 1024
TEMPLATES = 8


def with_ends(array, stream_key, low, high):
    extent = array.shape
    index_at = [jax.random.randint(jax.random.fold_in(stream_key, axis), (), 0, extent[axis]) for axis in range(len(extent))]
    array = array.at[tuple(index_at)].set(low)
    longest = extent.index(max(extent))
    index_at[longest] = (index_at[longest] + 1) % extent[longest]
    return array.at[tuple(index_at)].set(high)


def shard_levels(key, extent, cuts, least, largest):
    gain = 1.0
    for axis_at, shards_of in cuts:
        heights = jax.random.uniform(jax.random.fold_in(jax.random.fold_in(key, 6), axis_at), (shards_of,), jnp.float32, least / len(cuts), largest / len(cuts))
        gain = gain * jnp.repeat(jnp.exp(heights), extent[axis_at] // shards_of).reshape((-1,) + (1,) * (len(extent) - 1 - axis_at))
    return gain


def noise(own_key, extent, spread, limit, pieces=(), held_as=jnp.bfloat16):
    factor_of = shard_levels(own_key, extent, pieces, -0.22, 0.18) if pieces else 1.0
    entries = jax.random.normal(own_key, extent, jnp.float32) * spread * factor_of
    return jnp.minimum(jnp.maximum(entries, -limit), limit).astype(held_as)


def setup_inputs(seed: int = 0) -> dict:
    splits = jax.random.split(jax.random.key(seed), 5)
    strain = noise(splits[0], (2, DET, NLEN), 1.0, 6.0, ((2, 32),), jnp.float32)
    templates = noise(splits[1], (2, TEMPLATES, SPLIT, SPLIT), 1.0, 6.0, ((1, 8), (2, 32)), jnp.float32)
    pattern = with_ends((jax.random.randint(splits[2], (TEMPLATES, NFB), 0, 4) < 3).astype(jnp.int32), jax.random.fold_in(splits[2], 1), 0, 1)
    cutoff = with_ends(jax.random.randint(splits[3], (TEMPLATES,), NFB // 4, NFB + 1), jax.random.fold_in(splits[3], 1), NFB // 4, NFB).astype(jnp.int32)
    return dict(strain=strain, templates=templates, pattern=pattern, cutoff=cutoff)


EPSILON = 1e-06

def reference(strain, templates, pattern, cutoff):
    full_length = SPLIT * SPLIT
    spectrum_all = jnp.fft.fft(strain[0] + 1j * strain[1], axis=-1)
    template_bank = jnp.swapaxes(templates, 2, 3).reshape(2, TEMPLATES, full_length)
    reach = (jnp.arange(NFB, dtype=jnp.int32)[None, :] < cutoff[:, None]).astype(strain.dtype)
    active = pattern.astype(strain.dtype) * reach
    bin_block = jnp.arange(full_length, dtype=jnp.int32) // (SPLIT * BD)

    def filter_one(packed):
        real_t, imag_t, act_row = packed
        weight = act_row[bin_block]
        real_h = real_t * weight
        imag_h = imag_t * weight
        norm_sq = jnp.sum(real_h * real_h + imag_h * imag_h)
        product = spectrum_all * (real_h - 1j * imag_h)[None, :]
        series = jnp.fft.ifft(product, axis=-1) * full_length / jnp.sqrt(full_length * (norm_sq + EPSILON))
        return lax.optimization_barrier(jnp.sum(series.real ** 2 + series.imag ** 2, axis=0))
    snr_power = lax.map(filter_one, (template_bank[0], template_bank[1], active))
    return (snr_power, lax.optimization_barrier(jnp.max(snr_power, axis=0)))
```

```python
import functools
import math

import jax
import jax.numpy as jnp
import numpy as np
from jax import lax
from jax.experimental import pallas as pl
from jax.experimental.pallas import tpu as pltpu
from jax.sharding import PartitionSpec as P

EPSILON = 1e-06
SIDE = 2048
FULL = SIDE * SIDE
RANKS = 32
GROUPS = 8
F32 = jnp.float32
BF16 = jnp.bfloat16
VMEM_LIMIT = 56 * 1024 * 1024


def split_table(table):
    high = table.astype(np.float32).astype(jnp.bfloat16)
    low = (table - high.astype(np.float64)).astype(np.float32).astype(jnp.bfloat16)
    return np.stack((high, low))


def section_table(orient, copies):
    sample = np.arange(64)
    order = np.array([2 * (m % 32) + m // 32 for m in range(64)])
    theta = 2.0 * np.pi * np.outer(sample, order) / 64.0
    cosine, sine = np.cos(theta), orient * np.sin(theta)
    eye = np.eye(copies)
    whole = np.block([[np.kron(eye, cosine), np.kron(eye, sine)], [np.kron(eye, -sine), np.kron(eye, cosine)]])
    return split_table(whole)


def column_table():
    dl = np.arange(16)[:, None, None]
    dh = np.arange(128)[None, :, None]
    b = np.arange(128)[None, None, :]
    theta = 2.0 * np.pi * ((b * (dl + 16 * dh)) % SIDE) / SIDE
    cosine, sine = np.cos(theta), np.sin(theta)
    whole = np.concatenate(
        (np.concatenate((cosine, sine), axis=2), np.concatenate((-sine, cosine), axis=2)), axis=1
    )
    return np.swapaxes(split_table(whole), 0, 1)


def row_twiddle():
    theta = 2.0 * np.pi * np.outer(np.arange(32), np.arange(128) % 64) / SIDE
    return np.stack((np.cos(theta), np.sin(theta))).astype(np.float32)


def phases(first, second, orient):
    angle = (first * second % FULL).astype(F32) * (orient * 2.0 * math.pi / FULL)
    return jnp.stack((jnp.cos(angle), jnp.sin(angle)))


def times_unit(value, numer, denom, orient):
    re, im = value
    numer = numer % denom
    if numer == 0:
        return value
    if 8 * numer % denom == 0:
        eighth = 8 * numer // denom
        if eighth == 4:
            return -re, -im
        if eighth in (2, 6):
            return (-im, re) if (eighth == 2) == (orient > 0) else (im, -re)
    cosine = math.cos(2.0 * math.pi * numer / denom)
    sine = orient * math.sin(2.0 * math.pi * numer / denom)
    return re * cosine - im * sine, re * sine + im * cosine


def butterfly(values, orient):
    count = len(values)
    if count == 1:
        return values
    if count == 2:
        (ar, ai), (br, bi) = values
        return [(ar + br, ai + bi), (ar - br, ai - bi)]
    if count == 4:
        (ar, ai), (br, bi), (cr, ci), (dr, di) = values
        sr, si, tr, ti = ar + cr, ai + ci, ar - cr, ai - ci
        ur, ui, vr, vi = br + dr, bi + di, br - dr, bi - di
        if orient > 0:
            return [(sr + ur, si + ui), (tr - vi, ti + vr), (sr - ur, si - ui), (tr + vi, ti - vr)]
        return [(sr + ur, si + ui), (tr + vi, ti - vr), (sr - ur, si - ui), (tr - vi, ti + vr)]
    radix = 4 if count % 4 == 0 else 2
    inner = count // radix
    parts = [butterfly(values[s::radix], orient) for s in range(radix)]
    out = [None] * count
    for k in range(inner):
        joined = butterfly([times_unit(parts[s][k], s * k, count, orient) for s in range(radix)], orient)
        for part in range(radix):
            out[k + inner * part] = joined[part]
    return out


def halves(value):
    high = value.astype(BF16)
    return high, (value - high.astype(F32)).astype(BF16)


def dot(a, b, contract=((1,), (0,))):
    return lax.dot_general(a, b, (contract, ((), ())), preferred_element_type=F32)


def low_lanes(shape):
    return lax.broadcasted_iota(jnp.int32, shape, 1) < 64


def swap(value):
    return pltpu.roll(value, 64, 1)


def tile_rows(start):
    return pl.ds(pl.multiple_of(start, 8), 8)


def gather_columns(group_ref, strain_ref, out_ref):
    first = group_ref[0] * 4

    def piece(detector, tile, part):
        return strain_ref[pl.ds(detector * 2048 + first + tile * 2 + part, 64, stride=32), :]

    for tile in range(2):
        for at, (one, two) in enumerate((((0, 0), (1, 0)), ((0, 1), (1, 1)), ((2, 0), (2, 1)))):
            joined = jnp.concatenate((piece(one[0], tile, one[1]), piece(two[0], tile, two[1])), axis=0)
            out_ref[16 * tile:16 * tile + 16, 8 * at:8 * at + 8, :] = joined.T.reshape(16, 8, 128)


def prepare_templates(weight_ref, template_ref, out_ref, norm_ref):
    total = jnp.zeros((64, 128), F32)
    for chunk in range(16):
        lanes = slice(128 * chunk, 128 * chunk + 128)
        weight = weight_ref[:, lanes]
        for part in range(2):
            value = template_ref[part, :, lanes] * weight
            total = total + value * value
            out_ref[part, lanes, :] = jnp.concatenate((value, value), axis=0).T
    norm_ref[...] = jnp.sum(total.reshape(8, 8, 128), axis=0)


def first_section(in_ref, twiddle_ref, wide_ref, narrow_ref, phase_ref, out_ref, pair_ref, single_ref, turn_ref):
    lower = low_lanes((8, 128))
    for at in range(2):
        values = []
        for rank in range(RANKS):
            if at == 0:
                values.append((in_ref[rank, 0:8, :], in_ref[rank, 8:16, :]))
            else:
                one = in_ref[rank, 16:24, :]
                values.append((one, swap(one)))
        for digit, (re, im) in enumerate(butterfly(values, -1)):
            cosine, sine = twiddle_ref[0, digit:digit + 1, :], twiddle_ref[1, digit:digit + 1, :]
            re, im = re * cosine + im * sine, im * cosine - re * sine
            rows = slice(8 * digit, 8 * digit + 8)
            if at == 0:
                pair_ref[rows, 0:128] = re
                pair_ref[rows, 128:256] = im
            else:
                single_ref[rows, :] = jnp.where(lower, re, swap(im))
    high, low = halves(pair_ref[...])
    pair = dot(high, wide_ref[0]) + dot(low, wide_ref[0]) + dot(high, wide_ref[1])
    high, low = halves(single_ref[...])
    single = dot(high, narrow_ref[0]) + dot(low, narrow_ref[0]) + dot(high, narrow_ref[1])
    cosine, sine = phase_ref[0], phase_ref[1]
    re, im = pair[:, 0:128], pair[:, 128:256]
    turn_ref[0] = re * cosine - im * sine
    turn_ref[1] = im * cosine + re * sine
    turn_ref[2] = single * cosine + swap(single) * jnp.where(low_lanes((256, 128)), -sine, sine)
    for at in range(3):
        for quad in range(2):
            cols = [turn_ref[at, pl.ds(4 * quad + u, 32, stride=8), :] for u in range(4)]
            stacked = jnp.concatenate(
                [jnp.concatenate([c[:, 32 * s:32 * s + 32] for c in cols], axis=1) for s in range(4)], axis=0
            )
            turned = stacked.T
            for u in range(4):
                out_ref[pl.ds(8 * at + 4 * quad + u, 32, stride=24), :] = turned[32 * u:32 * u + 32, :]


def middle_section(in_ref, template_ref, near_ref, far_ref, table_hbm, out_ref, work_ref, table_ref, table_sem):
    copy = pltpu.make_async_copy(table_hbm, table_ref, table_sem)
    copy.start()

    def spread(low, carry):
        for at in range(2):
            values = []
            for a in range(16):
                rank = 16 * (a % 2) + low
                if at == 0:
                    values.append((in_ref[a // 2, rank, 0:8, :], in_ref[a // 2, rank, 8:16, :]))
                else:
                    one = in_ref[a // 2, rank, 16:24, :]
                    values.append((one, swap(one)))
            for digit, (re, im) in enumerate(butterfly(values, -1)):
                work_ref[digit, tile_rows(8 * low), 128 * at:128 * at + 128] = re
                work_ref[digit, tile_rows(128 + 8 * low), 128 * at:128 * at + 128] = im
        return carry

    lax.fori_loop(0, 16, spread, 0)
    copy.wait()

    def filter_digit(digit, carry):
        table_high, table_low = table_ref[digit, 0], table_ref[digit, 1]
        high, low = halves(work_ref[digit])
        spectrum = dot(table_high, high) + dot(table_high, low) + dot(table_low, high)
        h_re = template_ref[0, pl.ds(digit, 128, stride=16), :]
        h_im = template_ref[1, pl.ds(digit, 128, stride=16), :]
        h_re = jnp.concatenate((h_re, h_re), axis=1)
        h_im = jnp.concatenate((h_im, h_im), axis=1)
        s_re, s_im = spectrum[0:128], spectrum[128:256]
        product = jnp.concatenate((s_re * h_re + s_im * h_im, s_im * h_re - s_re * h_im), axis=0)
        high, low = halves(product)
        turn = ((0,), (0,))
        series = dot(table_high, high, turn) + dot(table_high, low, turn) + dot(table_low, high, turn)
        cosine = jnp.concatenate((near_ref[0], near_ref[0]), axis=1)
        sine = jnp.concatenate((near_ref[1], near_ref[1]), axis=1)
        re, im = series[0:128], series[128:256]
        work_ref[digit, 0:128, :] = re * cosine - im * sine
        work_ref[digit, 128:256, :] = re * sine + im * cosine
        return carry

    lax.fori_loop(0, 16, filter_digit, 0)
    lower = low_lanes((8, 128))

    def finish(values, row, part_rows, base, half):
        for digit, (re, im) in enumerate(butterfly(values, 1)):
            cosine, sine = far_ref[0, digit:digit + 1, :], far_ref[1, digit:digit + 1, :]
            out_ref[2 * digit + half, tile_rows(base + row), :] = re * cosine - im * sine
            out_ref[2 * digit + half, tile_rows(base + part_rows + row), :] = re * sine + im * cosine

    def collect_pair(step, carry):
        for half in range(2):
            rows = 64 * half + 8 * step
            values = [
                (work_ref[d, tile_rows(rows), 0:128], work_ref[d, tile_rows(128 + rows), 0:128]) for d in range(16)
            ]
            finish(values, 8 * step, 64, 0, half)
        return carry

    lax.fori_loop(0, 8, collect_pair, 0)

    def collect_single(step, carry):
        for half in range(2):
            rows = 64 * half + 8 * step
            values = []
            for d in range(16):
                both = []
                for part in range(2):
                    one = work_ref[d, tile_rows(128 * part + rows), 128:256]
                    two = work_ref[d, tile_rows(128 * part + rows + 32), 128:256]
                    both.append(jnp.where(lower, one, swap(two)))
                values.append(tuple(both))
            finish(values, 8 * step, 32, 128, half)
        return carry

    lax.fori_loop(0, 4, collect_single, 0)


def last_section(in_ref, twiddle_ref, wide_ref, norm_ref, out_ref, pair_ref, single_ref):
    def spread(work_ref, base, part_rows):
        def step_fn(step, carry):
            values = [
                (in_ref[r, tile_rows(base + 8 * step), :], in_ref[r, tile_rows(base + part_rows + 8 * step), :])
                for r in range(RANKS)
            ]
            for digit, (re, im) in enumerate(butterfly(values, 1)):
                cosine, sine = twiddle_ref[0, digit:digit + 1, :], twiddle_ref[1, digit:digit + 1, :]
                rows = tile_rows(part_rows * digit + 8 * step)
                work_ref[rows, 0:128] = re * cosine - im * sine
                work_ref[rows, 128:256] = im * cosine + re * sine
            return carry

        lax.fori_loop(0, part_rows // 8, step_fn, 0)

    spread(pair_ref, 0, 64)
    spread(single_ref, 128, 32)

    def power_of(value):
        high, low = halves(value)
        full = dot(high, wide_ref[0]) + dot(low, wide_ref[0]) + dot(high, wide_ref[1])
        re, im = full[:, 0:128], full[:, 128:256]
        return re * re + im * im

    lower = low_lanes((32, 128))

    def combine(quad, carry):
        pair = power_of(pair_ref[pl.ds(pl.multiple_of(256 * quad, 256), 256), :])
        single = power_of(single_ref[pl.ds(pl.multiple_of(128 * quad, 128), 128), :]).T
        for two in range(2):
            turned = pair[128 * two:128 * two + 128].T
            summed = turned[0:64] + turned[64:128]
            even, odd = summed[0:32], summed[32:64]
            both = (jnp.where(lower, even, swap(odd)), jnp.where(lower, swap(even), odd))
            for one in range(2):
                u = 2 * two + one
                lanes = slice(32 * u, 32 * u + 32)
                rest = jnp.concatenate(
                    (single[0:32, lanes], single[64:96, lanes], single[32:64, lanes], single[96:128, lanes]), axis=1
                )
                out_ref[pl.ds(4 * quad + u, 32, stride=40), :] = both[one] + rest
        return carry

    lax.fori_loop(0, 8, combine, 0)
    norm = norm_ref[...]
    for rank in range(RANKS):
        out_ref[40 * rank + 32:40 * rank + 40, :] = norm


def place_samples(in_ref, out_ref):
    total = jnp.zeros((8, 128), F32)
    for rank in range(RANKS):
        total = total + in_ref[rank, 32:40, :]
    scale = 1.0 / (FULL * (jnp.sum(total) + EPSILON))
    lower = low_lanes((32, 128))
    for two in range(16):
        one = in_ref[2 * two, 0:32, :] * scale
        other = in_ref[2 * two + 1, 0:32, :] * scale
        out_ref[pl.ds(two, 32, stride=16), :] = jnp.where(lower, one, swap(other))
        out_ref[pl.ds(512 + two, 32, stride=16), :] = jnp.where(lower, swap(one), other)


PARAMS = pltpu.CompilerParams(vmem_limit_bytes=VMEM_LIMIT)


def shape(*dims):
    return jax.ShapeDtypeStruct(dims, F32)


def call(kernel, out, specs, scratch=(), **kwargs):
    many = isinstance(out, (tuple, list))
    whole = pl.BlockSpec(memory_space=pltpu.VMEM)
    return pl.pallas_call(
        kernel,
        out_shape=out,
        in_specs=specs,
        out_specs=[whole] * len(out) if many else whole,
        scratch_shapes=list(scratch),
        compiler_params=PARAMS,
        **kwargs,
    )


def cost(us):
    return pl.CostEstimate(flops=int(us * 1e9), bytes_accessed=int(us * 1e6), transcendentals=0)


def group_peak(values):
    rows = values.shape[0]
    me = lax.axis_index("tmpl")
    core, y = me % 2, me // 2
    half, part = rows // 2, rows // 8
    across = [(i, i ^ 1) for i in range(GROUPS)]

    def around(step):
        return [(i, ((i // 2 + step) % 4) * 2 + i % 2) for i in range(GROUPS)]

    mine = lax.dynamic_slice_in_dim(values, core * half, half, 0)
    other = lax.dynamic_slice_in_dim(values, (1 - core) * half, half, 0)
    mine = jnp.maximum(mine, lax.ppermute(other, "tmpl", across))
    parts = mine.reshape(4, part, 128)
    got = [
        lax.ppermute(lax.dynamic_index_in_dim(parts, (y + s) % 4, 0, False), "tmpl", around(s)) for s in (1, 2, 3)
    ]
    best = lax.dynamic_index_in_dim(parts, y, 0, False)
    for one in got:
        best = jnp.maximum(best, one)
    spread = [best] + [lax.ppermute(best, "tmpl", around(s)) for s in (1, 2, 3)]
    full = jnp.zeros((4, part, 128), values.dtype)
    for step, one in enumerate(spread):
        full = lax.dynamic_update_index_in_dim(full, one, (y - step) % 4, 0)
    far = lax.ppermute(full, "tmpl", across)
    first = jnp.where(core == 0, full, far)
    second = jnp.where(core == 0, far, full)
    return jnp.concatenate((first, second), axis=0).reshape(rows, 128)


def local(strain, templates, pattern, cutoff):
    me = lax.axis_index("tm")
    group = lax.axis_index("tmpl")
    vmem = pl.BlockSpec(memory_space=pltpu.VMEM)
    smem = pl.BlockSpec(memory_space=pltpu.SMEM)
    anywhere = pl.BlockSpec(memory_space=pl.ANY)

    samples = strain.reshape(2, 3, 64, 16, 128).transpose(1, 2, 3, 0, 4).reshape(6144, 128)
    columns = call(gather_columns, shape(RANKS, 24, 128), [smem, vmem], cost_estimate=cost(3))(
        group.astype(jnp.int32).reshape(1), samples
    )
    columns = lax.all_to_all(columns, "tm", 0, 0, tiled=True)

    block_index = jnp.arange(pattern.shape[1], dtype=jnp.int32)
    active = pattern.astype(F32) * (block_index[None, :] < cutoff[:, None]).astype(F32)
    weight = jnp.repeat(active, SIDE // pattern.shape[1], axis=1)
    bank, norm = call(
        prepare_templates, (shape(2, SIDE, 128), shape(8, 128)), [vmem, vmem], cost_estimate=cost(4)
    )(weight, templates.reshape(2, 64, SIDE))

    row = jnp.arange(256, dtype=jnp.int32)[:, None]
    lane = jnp.arange(128, dtype=jnp.int32)[None, :]
    bin_at = row // 8 + 32 * (2 * (lane % 32) + lane // 32 % 2)
    first_phase = phases(256 * group + 8 * me + row % 8, bin_at, -1.0)
    bin_mine = 64 * me + lane % 64
    near = phases(jnp.arange(128, dtype=jnp.int32)[:, None], bin_mine, 1.0)
    far = phases(128 * jnp.arange(16, dtype=jnp.int32)[:, None], bin_mine, 1.0)
    twiddle = jnp.asarray(row_twiddle())

    rows = call(
        first_section,
        shape(RANKS * 24, 128),
        [vmem] * 5,
        [pltpu.VMEM((256, 256), F32), pltpu.VMEM((256, 128), F32), pltpu.VMEM((3, 256, 128), F32)],
        cost_estimate=cost(4),
    )(columns, twiddle, jnp.asarray(section_table(-1.0, 2)), jnp.asarray(section_table(-1.0, 1)), first_phase)
    rows = lax.all_to_all(rows.reshape(RANKS, 24, 128), "tm", 0, 0, tiled=True)
    rows = lax.all_gather(rows, "tmpl", axis=0)

    series = call(
        middle_section,
        shape(RANKS, 192, 128),
        [vmem] * 4 + [anywhere],
        [
            pltpu.VMEM((16, 256, 256), F32),
            pltpu.VMEM((16, 2, 256, 256), BF16),
            pltpu.SemaphoreType.DMA,
        ],
        cost_estimate=cost(10),
    )(rows, bank, near, far, jnp.asarray(column_table()))
    series = lax.all_to_all(series, "tm", 0, 0, tiled=True)

    power = call(
        last_section,
        shape(RANKS * 40, 128),
        [vmem] * 4,
        [pltpu.VMEM((2048, 256), F32), pltpu.VMEM((1024, 256), F32)],
        cost_estimate=cost(8),
    )(series, twiddle, jnp.asarray(section_table(1.0, 2)), norm)
    power = lax.all_to_all(power.reshape(RANKS, 40, 128), "tm", 0, 0, tiled=True)
    snr = call(place_samples, shape(1024, 128), [vmem], cost_estimate=cost(2))(power)
    peak = group_peak(snr)
    return snr.reshape(1, 64 * SIDE), peak.reshape(64 * SIDE)


def solution(mesh):
    in_specs = (P(None, None, "tm"), P(None, "tmpl", "tm", None), P("tmpl", None), P("tmpl"))
    out_specs = (P("tmpl", "tm"), P("tm"))
    return jax.shard_map(local, mesh=mesh, in_specs=in_specs, out_specs=out_specs, check_vma=False)
```

```python
import functools
import math

import jax
import jax.numpy as jnp
import numpy as np
from jax import lax
from jax.experimental import pallas as pl
from jax.experimental.pallas import tpu as pltpu
from jax.sharding import PartitionSpec as P

EPSILON = 1e-06
SIDE = 2048
FULL = SIDE * SIDE
DETECTORS = 3
MESSAGE = 33
RANKS = 32
GROUPS = 8
F32 = jnp.float32
BF16 = jnp.bfloat16
VMEM_LIMIT = 56 * 1024 * 1024


def split_table(table):
    high = table.astype(np.float32).astype(jnp.bfloat16)
    low = (table - high.astype(np.float64)).astype(np.float32).astype(jnp.bfloat16)
    return np.stack((high, low))


def section_table(orient, copies):
    sample = np.arange(64)
    order = np.array([2 * (m % 32) + m // 32 for m in range(64)])
    theta = 2.0 * np.pi * np.outer(sample, order) / 64.0
    cosine, sine = np.cos(theta), orient * np.sin(theta)
    eye = np.eye(copies)
    whole = np.block([[np.kron(eye, cosine), np.kron(eye, sine)], [np.kron(eye, -sine), np.kron(eye, cosine)]])
    return split_table(whole)


def column_table():
    theta = 2.0 * np.pi * np.outer(np.arange(128), np.arange(128)) / 128.0
    cosine, sine = np.cos(theta), np.sin(theta)
    whole = np.block([[cosine, sine], [-sine, cosine]])
    return np.stack((split_table(whole), split_table(whole.T)))


def digit_twiddle():
    digit = 2 * np.arange(8)[:, None, None] + (np.arange(128) // 64)[None, None, :]
    theta = 2.0 * np.pi * (np.arange(128)[None, :, None] * digit) / SIDE
    return np.stack((np.cos(theta), np.sin(theta)), axis=1).astype(np.float32)


def fold_twiddle():
    theta = 2.0 * np.pi * np.outer(np.arange(8), np.arange(128) // 64) / 16.0
    return np.stack((np.cos(theta), -np.sin(theta)), axis=1).astype(np.float32)


def row_twiddle():
    theta = 2.0 * np.pi * np.outer(np.arange(32), np.arange(128) % 64) / SIDE
    return np.stack((np.cos(theta), np.sin(theta))).astype(np.float32)


def phases(first, second, orient):
    angle = (first * second % FULL).astype(F32) * (orient * 2.0 * math.pi / FULL)
    return jnp.stack((jnp.cos(angle), jnp.sin(angle)))


def times_unit(value, numer, denom, orient):
    re, im = value
    numer = numer % denom
    if numer == 0:
        return value
    if 8 * numer % denom == 0:
        eighth = 8 * numer // denom
        if eighth == 4:
            return -re, -im
        if eighth in (2, 6):
            return (-im, re) if (eighth == 2) == (orient > 0) else (im, -re)
    cosine = math.cos(2.0 * math.pi * numer / denom)
    sine = orient * math.sin(2.0 * math.pi * numer / denom)
    return re * cosine - im * sine, re * sine + im * cosine


def butterfly(values, orient):
    count = len(values)
    if count == 1:
        return values
    if count == 2:
        (ar, ai), (br, bi) = values
        return [(ar + br, ai + bi), (ar - br, ai - bi)]
    if count == 4:
        (ar, ai), (br, bi), (cr, ci), (dr, di) = values
        sr, si, tr, ti = ar + cr, ai + ci, ar - cr, ai - ci
        ur, ui, vr, vi = br + dr, bi + di, br - dr, bi - di
        if orient > 0:
            return [(sr + ur, si + ui), (tr - vi, ti + vr), (sr - ur, si - ui), (tr + vi, ti - vr)]
        return [(sr + ur, si + ui), (tr + vi, ti - vr), (sr - ur, si - ui), (tr - vi, ti + vr)]
    radix = 4 if count % 4 == 0 else 2
    inner = count // radix
    parts = [butterfly(values[s::radix], orient) for s in range(radix)]
    out = [None] * count
    for k in range(inner):
        joined = butterfly([times_unit(parts[s][k], s * k, count, orient) for s in range(radix)], orient)
        for part in range(radix):
            out[k + inner * part] = joined[part]
    return out


def halves(value):
    high = value.astype(BF16)
    return high, (value - high.astype(F32)).astype(BF16)


def dot(a, b, contract=((1,), (0,))):
    return lax.dot_general(a, b, (contract, ((), ())), preferred_element_type=F32)


def low_lanes(shape):
    return lax.broadcasted_iota(jnp.int32, shape, 1) < 64


def swap(value):
    return pltpu.roll(value, 64, 1)


def tile_rows(start):
    return pl.ds(pl.multiple_of(start, 8), 8)


def gather_columns(group_ref, strain_ref, out_ref):
    first = 4 * lax.rem(group_ref[0], 2)

    def piece(detector, tile, part):
        return strain_ref[pl.ds(512 * detector + first + 2 * tile + part, 64, stride=8), :]

    for tile in range(2):
        for at, (one, two) in enumerate((((0, 0), (1, 0)), ((0, 1), (1, 1)), ((2, 0), (2, 1)))):
            joined = jnp.concatenate((piece(one[0], tile, one[1]), piece(two[0], tile, two[1])), axis=0)
            out_ref[16 * tile:16 * tile + 16, 8 * at:8 * at + 8, :] = joined.T.reshape(16, 8, 128)


def prepare_templates(weight_ref, template_ref, out_ref, norm_ref):
    total = jnp.zeros((64, 128), F32)
    for chunk in range(16):
        lanes = slice(128 * chunk, 128 * chunk + 128)
        weight = weight_ref[:, lanes]
        for part in range(2):
            value = template_ref[part, :, lanes] * weight
            total = total + value * value
            out_ref[part, lanes, :] = jnp.concatenate((value, pltpu.roll(value, 127, 1)), axis=0).T
    norm_ref[...] = jnp.sum(total.reshape(8, 8, 128), axis=0)


def first_section(in_ref, twiddle_ref, wide_ref, narrow_ref, phase_ref, out_ref, pair_ref, single_ref, turn_ref):
    lower = low_lanes((8, 128))
    for at in range(2):
        values = []
        for rank in range(RANKS):
            if at == 0:
                values.append((in_ref[rank, 0:8, :], in_ref[rank, 8:16, :]))
            else:
                one = in_ref[rank, 16:24, :]
                values.append((one, swap(one)))
        for digit, (re, im) in enumerate(butterfly(values, -1)):
            cosine, sine = twiddle_ref[0, digit:digit + 1, :], twiddle_ref[1, digit:digit + 1, :]
            re, im = re * cosine + im * sine, im * cosine - re * sine
            rows = slice(8 * digit, 8 * digit + 8)
            if at == 0:
                pair_ref[rows, 0:128] = re
                pair_ref[rows, 128:256] = im
            else:
                single_ref[rows, :] = jnp.where(lower, re, swap(im))
    high, low = halves(pair_ref[...])
    pair = dot(high, wide_ref[0]) + dot(low, wide_ref[0]) + dot(high, wide_ref[1])
    high, low = halves(single_ref[...])
    single = dot(high, narrow_ref[0]) + dot(low, narrow_ref[0]) + dot(high, narrow_ref[1])
    cosine, sine = phase_ref[0], phase_ref[1]
    re, im = pair[:, 0:128], pair[:, 128:256]
    turn_ref[0] = re * cosine - im * sine
    turn_ref[1] = im * cosine + re * sine
    turn_ref[2] = single * cosine + swap(single) * jnp.where(low_lanes((256, 128)), -sine, sine)
    for at in range(DETECTORS):
        for quad in range(2):
            blocks = []
            for part in range(2):
                source, start = (part, 64 * at) if at < 2 else (2, 64 * part)
                cols = [turn_ref[source, pl.ds(4 * quad + u, 32, stride=8), :] for u in range(4)]
                for odd in range(2):
                    lanes = slice(start + 32 * odd, start + 32 * odd + 32)
                    blocks.append(jnp.concatenate([c[:, lanes] for c in cols], axis=1))
            turned = jnp.concatenate(blocks, axis=0).T
            for u in range(4):
                out_ref[pl.ds(8 * at + 4 * quad + u, 32, stride=24), :] = turned[32 * u:32 * u + 32, :]


def filter_detector(load, template_ref, near_ref, far_ref, table_ref, digit_ref, fold_ref, out_ref, base, work_ref):
    lower = low_lanes((8, 128))

    def spread(low, carry):
        values = []
        for a in range(8):
            one = load(a // 2, 16 * (a % 2) + low)
            two = load(a // 2 + 4, 16 * (a % 2) + low)
            add, sub = one + two, one - two
            re, im = jnp.where(lower, add, swap(sub)), jnp.where(lower, swap(add), sub)
            cosine, sine = fold_ref[a, 0:1, :], fold_ref[a, 1:2, :]
            values.append((re * cosine - im * sine, re * sine + im * cosine) if a else (re, im))
        for pair, (re, im) in enumerate(butterfly(values, -1)):
            cosine, sine = digit_ref[pair, 0, tile_rows(8 * low), :], digit_ref[pair, 1, tile_rows(8 * low), :]
            lanes = slice(128 * (pair % 2), 128 * (pair % 2) + 128)
            work_ref[pair // 2, tile_rows(8 * low), lanes] = re * cosine + im * sine
            work_ref[pair // 2, tile_rows(128 + 8 * low), lanes] = im * cosine - re * sine
        return carry

    lax.fori_loop(0, 16, spread, 0)

    for quad in range(4):
        high, low = halves(work_ref[quad])
        spectrum = dot(table_ref[0, 0], high) + dot(table_ref[0, 0], low) + dot(table_ref[0, 1], high)
        s_re, s_im = spectrum[0:128], spectrum[128:256]
        rows = [pl.ds(4 * quad + 2 * k, 128, stride=16) for k in range(2)]
        h_re = jnp.concatenate([template_ref[0, r, :] for r in rows], axis=1)
        h_im = jnp.concatenate([template_ref[1, r, :] for r in rows], axis=1)
        product = jnp.concatenate((s_re * h_re + s_im * h_im, s_im * h_re - s_re * h_im), axis=0)
        high, low = halves(product)
        series = dot(table_ref[1, 0], high) + dot(table_ref[1, 0], low) + dot(table_ref[1, 1], high)
        for k in range(2):
            lanes = slice(128 * k, 128 * k + 128)
            re, im = series[0:128, lanes], series[128:256, lanes]
            cosine, sine = digit_ref[2 * quad + k, 0], digit_ref[2 * quad + k, 1]
            re, im = re * cosine - im * sine, re * sine + im * cosine
            cosine, sine = near_ref[0], near_ref[1]
            work_ref[quad, 0:128, lanes] = re * cosine - im * sine
            work_ref[quad, 128:256, lanes] = re * sine + im * cosine

    def collect(step, carry):
        for half in range(2):
            tiles = []
            for shift in (0, 32):
                rows = 64 * half + 8 * step + shift
                values = []
                for pair in range(8):
                    lanes = slice(128 * (pair % 2), 128 * (pair % 2) + 128)
                    values.append(
                        (work_ref[pair // 2, tile_rows(rows), lanes], work_ref[pair // 2, tile_rows(128 + rows), lanes])
                    )
                tiles.append(butterfly(values, 1))
            for digit in range(8):
                one, two = tiles[0][digit], tiles[1][digit]
                even = [jnp.where(lower, one[p], swap(two[p])) for p in range(2)]
                odd = [jnp.where(lower, swap(one[p]), two[p]) for p in range(2)]
                for high, (re, im) in enumerate(butterfly([tuple(even), times_unit(tuple(odd), digit, 16, 1)], 1)):
                    block = digit + 8 * high
                    cosine, sine = far_ref[0, block:block + 1, :], far_ref[1, block:block + 1, :]
                    out_ref[2 * block + half, tile_rows(base + 8 * step), :] = re * cosine - im * sine
                    out_ref[2 * block + half, tile_rows(base + 32 + 8 * step), :] = re * sine + im * cosine
        return carry

    lax.fori_loop(0, 4, collect, 0)


def filter_first(group_ref, *refs):
    pieces, tables, (out_ref, work_ref, held_ref, sems) = refs[:8], refs[8:14], refs[14:]
    core, y = lax.rem(group_ref[0], 2), lax.div(group_ref[0], 2)
    copies = []
    for at, piece in enumerate(pieces):
        side = core if at < 4 else 1 - core
        slot = 2 * lax.rem(y + (4 - at % 4), 4) + side
        copy = pltpu.make_async_copy(piece, held_ref.at[slot], sems.at[at])
        copy.start()
        copies.append(copy)
    for copy in copies:
        copy.wait()
    filter_detector(lambda group, rank: held_ref[group, rank], *tables, out_ref, 0, work_ref)


def filter_rest(in_ref, *refs):
    tables, (out_ref, work_ref) = refs[:6], refs[6:]
    for at in range(2):
        filter_detector(
            lambda group, rank, rows=slice(8 * at, 8 * at + 8): in_ref[group, rank, rows, :],
            *tables, out_ref, 64 * at, work_ref,
        )


def detector_power(in_ref, base, twiddle_ref, wide_ref, work_ref):
    def step_fn(step, carry):
        values = [
            (in_ref[r, tile_rows(base + 8 * step), :], in_ref[r, tile_rows(base + 32 + 8 * step), :])
            for r in range(RANKS)
        ]
        for digit, (re, im) in enumerate(butterfly(values, 1)):
            cosine, sine = twiddle_ref[0, digit:digit + 1, :], twiddle_ref[1, digit:digit + 1, :]
            rows = tile_rows(32 * digit + 8 * step)
            work_ref[rows, 0:128] = re * cosine - im * sine
            work_ref[rows, 128:256] = im * cosine + re * sine
        return carry

    lax.fori_loop(0, 4, step_fn, 0)

    def power_of(quad):
        high, low = halves(work_ref[pl.ds(pl.multiple_of(128 * quad, 128), 128), :])
        full = dot(high, wide_ref[0]) + dot(low, wide_ref[0]) + dot(high, wide_ref[1])
        re, im = full[:, 0:128], full[:, 128:256]
        return re * re + im * im

    return power_of


def start_power(in_ref, twiddle_ref, wide_ref, out_ref, work_ref):
    power_of = detector_power(in_ref, 0, twiddle_ref, wide_ref, work_ref)

    def step_fn(quad, carry):
        out_ref[pl.ds(pl.multiple_of(128 * quad, 128), 128), :] = power_of(quad)
        return carry

    lax.fori_loop(0, 8, step_fn, 0)


def finish_power(in_ref, twiddle_ref, wide_ref, sum_ref, norm_ref, out_ref, one_ref, two_ref):
    first = detector_power(in_ref, 0, twiddle_ref, wide_ref, one_ref)
    second = detector_power(in_ref, 64, twiddle_ref, wide_ref, two_ref)

    def step_fn(quad, carry):
        rows = pl.ds(pl.multiple_of(128 * quad, 128), 128)
        turned = (first(quad) + second(quad) + sum_ref[rows, :]).T
        for u in range(4):
            lanes = slice(32 * u, 32 * u + 32)
            out_ref[pl.ds(4 * quad + u, 32, stride=MESSAGE), :] = jnp.concatenate(
                (turned[0:32, lanes], turned[64:96, lanes], turned[32:64, lanes], turned[96:128, lanes]), axis=1
            )
        return carry

    lax.fori_loop(0, 8, step_fn, 0)
    norm = jnp.sum(norm_ref[...], axis=0, keepdims=True)
    for rank in range(RANKS):
        out_ref[MESSAGE * rank + 32:MESSAGE * rank + 33, :] = norm


def place_samples(group_ref, in_ref, out_ref, keep_ref, send_ref):
    total = jnp.zeros((1, 128), F32)
    for rank in range(RANKS):
        total = total + in_ref[MESSAGE * rank + 32:MESSAGE * rank + 33, :]
    scale = 1.0 / (FULL * (jnp.sum(total) + EPSILON))
    lower = low_lanes((32, 128))
    zero = lax.rem(group_ref[0], 2) == 0
    for two in range(16):
        one = in_ref[2 * MESSAGE * two:2 * MESSAGE * two + 32, :] * scale
        other = in_ref[2 * MESSAGE * two + MESSAGE:2 * MESSAGE * two + MESSAGE + 32, :] * scale
        first, second = jnp.where(lower, one, swap(other)), jnp.where(lower, swap(one), other)
        rows = pl.ds(two, 32, stride=16)
        out_ref[rows, :] = first
        out_ref[pl.ds(512 + two, 32, stride=16), :] = second
        keep_ref[rows, :] = jnp.where(zero, first, second)
        send_ref[rows, :] = jnp.where(zero, second, first)


PARAMS = pltpu.CompilerParams(vmem_limit_bytes=VMEM_LIMIT)


def shape(*dims):
    return jax.ShapeDtypeStruct(dims, F32)


def call(kernel, out, specs, scratch=(), **kwargs):
    many = isinstance(out, (tuple, list))
    whole = pl.BlockSpec(memory_space=pltpu.VMEM)
    return pl.pallas_call(
        kernel,
        out_shape=out,
        in_specs=specs,
        out_specs=[whole] * len(out) if many else whole,
        scratch_shapes=list(scratch),
        compiler_params=PARAMS,
        **kwargs,
    )


def cost(us):
    return pl.CostEstimate(flops=int(us * 1e9), bytes_accessed=int(us * 1e6), transcendentals=0)


ACROSS = [(i, i ^ 1) for i in range(GROUPS)]


def around(step):
    return [(i, ((i // 2 + step) % 4) * 2 + i % 2) for i in range(GROUPS)]


def group_pieces(value):
    own = [value] + [lax.ppermute(value, "tmpl", around(step)) for step in (1, 2, 3)]
    return own + [lax.ppermute(one, "tmpl", ACROSS) for one in own]


def group_peak(keep, send):
    best = jnp.maximum(keep, lax.ppermute(send, "tmpl", ACROSS))
    got = [lax.ppermute(best, "tmpl", around(step)) for step in (1, 2, 3)]
    best = jnp.maximum(jnp.maximum(best, got[0]), jnp.maximum(got[1], got[2]))
    far = lax.ppermute(best, "tmpl", ACROSS)
    zero = lax.axis_index("tmpl") % 2 == 0
    return jnp.concatenate((jnp.where(zero, best, far), jnp.where(zero, far, best)), axis=0)


def local(strain, templates, pattern, cutoff):
    me = lax.axis_index("tm")
    group = lax.axis_index("tmpl")
    vmem = pl.BlockSpec(memory_space=pltpu.VMEM)
    smem = pl.BlockSpec(memory_space=pltpu.SMEM)
    anywhere = pl.BlockSpec(memory_space=pl.ANY)

    member = group.astype(jnp.int32).reshape(1)
    samples = strain.reshape(2, 3, 64, 16, 128).transpose(1, 2, 3, 0, 4).reshape(192, 32, 128)
    columns = pl.pallas_call(
        lambda group_ref, strain_ref, out_ref: gather_columns(group_ref, strain_ref.reshape(1536, 128), out_ref),
        out_shape=shape(RANKS, 24, 128),
        grid_spec=pltpu.PrefetchScalarGridSpec(
            num_scalar_prefetch=1,
            grid=(1,),
            in_specs=[pl.BlockSpec((192, 8, 128), lambda i, at: (0, at[0] // 2, 0))],
            out_specs=pl.BlockSpec((RANKS, 24, 128), lambda i, at: (0, 0, 0)),
        ),
        compiler_params=PARAMS,
        cost_estimate=cost(3),
    )(member, samples)
    columns = lax.all_to_all(columns, "tm", 0, 0, tiled=True)

    block_index = jnp.arange(pattern.shape[1], dtype=jnp.int32)
    active = pattern.astype(F32) * (block_index[None, :] < cutoff[:, None]).astype(F32)
    weight = jnp.repeat(active, SIDE // pattern.shape[1], axis=1)
    bank, norm = call(
        prepare_templates, (shape(2, SIDE, 128), shape(8, 128)), [vmem, vmem], cost_estimate=cost(4)
    )(weight, templates.reshape(2, 64, SIDE))

    row = jnp.arange(256, dtype=jnp.int32)[:, None]
    lane = jnp.arange(128, dtype=jnp.int32)[None, :]
    bin_at = row // 8 + 32 * (2 * (lane % 32) + lane // 32 % 2)
    first_phase = phases(256 * group + 8 * me + row % 8, bin_at, -1.0)
    bin_mine = 64 * me + lane % 64
    near = phases(jnp.arange(128, dtype=jnp.int32)[:, None], bin_mine, 1.0)
    far = phases(128 * jnp.arange(16, dtype=jnp.int32)[:, None], bin_mine, 1.0)
    twiddle = jnp.asarray(row_twiddle())

    columns, bank, norm, near, far, first_phase = lax.optimization_barrier(
        (columns, bank, norm, near, far, first_phase)
    )
    rows = call(
        first_section,
        shape(RANKS * 24, 128),
        [vmem] * 5,
        [pltpu.VMEM((256, 256), F32), pltpu.VMEM((256, 128), F32), pltpu.VMEM((3, 256, 128), F32)],
        cost_estimate=cost(4),
    )(columns, twiddle, jnp.asarray(section_table(-1.0, 2)), jnp.asarray(section_table(-1.0, 1)), first_phase)
    rows = lax.all_to_all(rows.reshape(RANKS, 24, 128), "tm", 0, 0, tiled=True)
    tables = [jnp.asarray(t) for t in (column_table(), digit_twiddle(), fold_twiddle())]
    wide = jnp.asarray(section_table(1.0, 2))
    others = lax.all_gather(rows[:, 0:16, :], "tmpl", axis=0)
    pieces = group_pieces(rows[:, 16:24, :])
    first = call(
        filter_first,
        shape(RANKS, 64, 128),
        [smem] + [anywhere] * 8 + [vmem] * 6,
        [pltpu.VMEM((4, 256, 256), F32), pltpu.VMEM((GROUPS, RANKS, 8, 128), F32), pltpu.SemaphoreType.DMA((8,))],
        cost_estimate=cost(8),
    )(member, *pieces, bank, near, far, *tables)
    first = lax.all_to_all(first, "tm", 0, 0, tiled=True)
    second = call(
        filter_rest, shape(RANKS, 128, 128), [vmem] * 7, [pltpu.VMEM((4, 256, 256), F32)], cost_estimate=cost(12)
    )(others, bank, near, far, *tables)
    second = lax.all_to_all(second, "tm", 0, 0, tiled=True)

    work = pltpu.VMEM((1024, 256), F32)
    total = call(start_power, shape(1024, 128), [vmem] * 3, [work], cost_estimate=cost(3))(first, twiddle, wide)
    power = call(finish_power, shape(RANKS * MESSAGE, 128), [vmem] * 5, [work] * 2, cost_estimate=cost(6))(
        second, twiddle, wide, total, norm
    )
    power = lax.all_to_all(power.reshape(RANKS, 1, MESSAGE * 128), "tm", 0, 0, tiled=True)
    power = power.reshape(RANKS * MESSAGE, 128)
    snr, keep, send = call(
        place_samples, (shape(1024, 128), shape(512, 128), shape(512, 128)), [smem, vmem], cost_estimate=cost(2)
    )(member, power)
    peak = group_peak(keep, send)
    return snr.reshape(1, 64 * SIDE), peak.reshape(64 * SIDE)


def solution(mesh):
    in_specs = (P(None, None, "tm"), P(None, "tmpl", "tm", None), P("tmpl", None), P("tmpl"))
    out_specs = (P("tmpl", "tm"), P("tm"))
    return jax.shard_map(local, mesh=mesh, in_specs=in_specs, out_specs=out_specs, check_vma=False)
```

```python
import functools
import math

import jax
import jax.numpy as jnp
import numpy as np
from jax import lax
from jax.experimental import pallas as pl
from jax.experimental.pallas import tpu as pltpu
from jax.sharding import PartitionSpec as P

EPSILON = 1e-06
SIDE = 2048
FULL = SIDE * SIDE
DETECTORS = 3
RANKS = 32
GROUPS = 8
F32 = jnp.float32
BF16 = jnp.bfloat16
VMEM_LIMIT = 56 * 1024 * 1024


def split_table(table):
    high = table.astype(np.float32).astype(jnp.bfloat16)
    low = (table - high.astype(np.float64)).astype(np.float32).astype(jnp.bfloat16)
    return np.stack((high, low))


def first_table(copies):
    theta = 2.0 * np.pi * np.outer(np.arange(64), np.arange(64)) / 64.0
    eye = np.eye(copies)
    cosine, sine = np.kron(eye, np.cos(theta)), np.kron(eye, np.sin(theta))
    return split_table(np.block([[cosine, -sine], [sine, cosine]]))


def last_table():
    theta = 2.0 * np.pi * np.outer(np.arange(16), np.arange(16)) / 16.0
    eye = np.eye(8)
    cosine, sine = np.kron(eye, np.cos(theta)), np.kron(eye, np.sin(theta))
    return split_table(np.block([[cosine, sine], [-sine, cosine]]))


def column_table():
    theta = 2.0 * np.pi * np.outer(np.arange(128), np.arange(128)) / 128.0
    cosine, sine = np.cos(theta), np.sin(theta)
    whole = np.block([[cosine, sine], [-sine, cosine]])
    return np.stack((split_table(whole), split_table(whole.T)))


def digit_twiddle():
    digit = 2 * np.arange(8)[:, None, None] + (np.arange(128) // 64)[None, None, :]
    theta = 2.0 * np.pi * (np.arange(128)[None, :, None] * digit) / SIDE
    return np.stack((np.cos(theta), np.sin(theta)), axis=1).astype(np.float32)


def fold_twiddle():
    theta = 2.0 * np.pi * np.outer(np.arange(8), np.arange(128) // 64) / 16.0
    return np.stack((np.cos(theta), -np.sin(theta)), axis=1).astype(np.float32)


def row_twiddle():
    theta = 2.0 * np.pi * np.outer(np.arange(32), np.arange(128) % 64) / SIDE
    return np.stack((np.cos(theta), np.sin(theta))).astype(np.float32)


def inner_twiddle():
    theta = 2.0 * np.pi * np.outer(np.arange(32), np.arange(128) % 16) / 512.0
    return np.stack((np.cos(theta), np.sin(theta))).astype(np.float32)


def phases(turns, orient):
    angle = (turns % FULL).astype(F32) * (orient * 2.0 * math.pi / FULL)
    return jnp.stack((jnp.cos(angle), jnp.sin(angle)))


def mixing_tables(place):
    k = jnp.arange(8, dtype=jnp.int32)[:, None, None]
    into = jnp.arange(128, dtype=jnp.int32)[None, :, None]
    out = jnp.arange(128, dtype=jnp.int32)[None, None, :]
    block, w = k + 8 * (out // 64), out // 16 % 4
    e, a, i = into // 64, into // 16 % 4, into % 16
    turns = e * block * (FULL // 16) + 128 * block * (512 * a + 16 * place + i)
    turns = turns % FULL + a * w * (FULL // 4) + (16 * place + i) * w * SIDE
    cosine, sine = phases(turns, 1.0) * (i == out % 16).astype(F32)
    whole = jnp.concatenate(
        (jnp.concatenate((cosine, sine), axis=2), jnp.concatenate((-sine, cosine), axis=2)), axis=1
    )
    high = lax.reduce_precision(whole, 8, 7)
    return jnp.stack((high.astype(BF16), (whole - high).astype(BF16)))


def times_unit(value, numer, denom, orient):
    re, im = value
    numer = numer % denom
    if numer == 0:
        return value
    if 8 * numer % denom == 0:
        eighth = 8 * numer // denom
        if eighth == 4:
            return -re, -im
        if eighth in (2, 6):
            return (-im, re) if (eighth == 2) == (orient > 0) else (im, -re)
    cosine = math.cos(2.0 * math.pi * numer / denom)
    sine = orient * math.sin(2.0 * math.pi * numer / denom)
    return re * cosine - im * sine, re * sine + im * cosine


def butterfly(values, orient):
    count = len(values)
    if count == 1:
        return values
    if count == 2:
        (ar, ai), (br, bi) = values
        return [(ar + br, ai + bi), (ar - br, ai - bi)]
    if count == 4:
        (ar, ai), (br, bi), (cr, ci), (dr, di) = values
        sr, si, tr, ti = ar + cr, ai + ci, ar - cr, ai - ci
        ur, ui, vr, vi = br + dr, bi + di, br - dr, bi - di
        if orient > 0:
            return [(sr + ur, si + ui), (tr - vi, ti + vr), (sr - ur, si - ui), (tr + vi, ti - vr)]
        return [(sr + ur, si + ui), (tr + vi, ti - vr), (sr - ur, si - ui), (tr - vi, ti + vr)]
    radix = 4 if count % 4 == 0 else 2
    inner = count // radix
    parts = [butterfly(values[s::radix], orient) for s in range(radix)]
    out = [None] * count
    for k in range(inner):
        joined = butterfly([times_unit(parts[s][k], s * k, count, orient) for s in range(radix)], orient)
        for part in range(radix):
            out[k + inner * part] = joined[part]
    return out


def halves(value):
    high = value.astype(BF16)
    return high, (value - high.astype(F32)).astype(BF16)


def dot(a, b, contract=((1,), (0,))):
    return lax.dot_general(a, b, (contract, ((), ())), preferred_element_type=F32)


def low_lanes(shape):
    return lax.broadcasted_iota(jnp.int32, shape, 1) < 64


def swap(value):
    return pltpu.roll(value, 64, 1)


def tile_rows(start):
    return pl.ds(pl.multiple_of(start, 8), 8)


def gather_columns(group_ref, strain_ref, out_ref):
    first = 4 * lax.rem(group_ref[0], 2)

    def piece(detector, tile, part):
        return strain_ref[pl.ds(512 * detector + first + 2 * tile + part, 64, stride=8), :]

    for tile in range(2):
        for at, (one, two) in enumerate((((0, 0), (1, 0)), ((0, 1), (1, 1)), ((2, 0), (2, 1)))):
            joined = jnp.concatenate((piece(one[0], tile, one[1]), piece(two[0], tile, two[1])), axis=0)
            out_ref[16 * tile:16 * tile + 16, 8 * at:8 * at + 8, :] = joined.T.reshape(16, 8, 128)


def prepare_templates(side_ref, *refs):
    pieces, (out_ref, norm_ref, held_ref, sems) = refs[:4], refs[4:]
    copies = []
    for at, piece in enumerate(pieces):
        copy = pltpu.make_async_copy(piece, held_ref.at[lax.rem(side_ref[0] + (4 - at), 4)], sems.at[at])
        copy.start()
        copies.append(copy)
    for copy in copies:
        copy.wait()
    total = jnp.zeros((64, 128), F32)
    for chunk in range(16):
        lanes = slice(128 * chunk, 128 * chunk + 128)
        for part in range(2):
            value = jnp.concatenate([held_ref[a, part, :, lanes] for a in range(4)], axis=0)
            total = total + value * value
            out_ref[part, lanes, :] = jnp.concatenate((value, pltpu.roll(value, 127, 1)), axis=0).T
    norm_ref[...] = jnp.sum(total.reshape(8, 8, 128), axis=0)


def first_section(in_ref, twiddle_ref, wide_ref, narrow_ref, phase_ref, out_ref, pair_ref, single_ref, turn_ref):
    lower = low_lanes((8, 128))
    for at in range(2):
        values = []
        for rank in range(RANKS):
            if at == 0:
                values.append((in_ref[rank, 0:8, :], in_ref[rank, 8:16, :]))
            else:
                one = in_ref[rank, 16:24, :]
                values.append((one, swap(one)))
        for digit, (re, im) in enumerate(butterfly(values, -1)):
            cosine, sine = twiddle_ref[0, digit:digit + 1, :], twiddle_ref[1, digit:digit + 1, :]
            re, im = re * cosine + im * sine, im * cosine - re * sine
            rows = slice(8 * digit, 8 * digit + 8)
            if at == 0:
                pair_ref[rows, 0:128] = re
                pair_ref[rows, 128:256] = im
            else:
                single_ref[rows, :] = jnp.where(lower, re, swap(im))
    high, low = halves(pair_ref[...])
    pair = dot(high, wide_ref[0]) + dot(low, wide_ref[0]) + dot(high, wide_ref[1])
    high, low = halves(single_ref[...])
    single = dot(high, narrow_ref[0]) + dot(low, narrow_ref[0]) + dot(high, narrow_ref[1])
    cosine, sine = phase_ref[0], phase_ref[1]
    re, im = pair[:, 0:128], pair[:, 128:256]
    turn_ref[0] = re * cosine - im * sine
    turn_ref[1] = im * cosine + re * sine
    turn_ref[2] = single * cosine + swap(single) * jnp.where(low_lanes((256, 128)), -sine, sine)
    for at in range(DETECTORS):
        for quad in range(2):
            blocks = []
            for part in range(2):
                source, start = (part, 64 * at) if at < 2 else (2, 64 * part)
                cols = [turn_ref[source, pl.ds(4 * quad + u, 32, stride=8), :] for u in range(4)]
                for a in range(4):
                    lanes = slice(start + 16 * a, start + 16 * a + 16)
                    blocks.append(jnp.concatenate([c[16 * h:16 * h + 16, lanes] for c in cols for h in range(2)], axis=1))
            turned = jnp.concatenate(blocks, axis=0).T
            for u in range(4):
                for h in range(2):
                    rows = pl.ds(24 * h + 8 * at + 4 * quad + u, 16, stride=48)
                    out_ref[rows, :] = turned[32 * u + 16 * h:32 * u + 16 * h + 16, :]


def slot_of(a, low):
    return 4 * (a % 2) + 2 * (low // 8) + a // 2 % 2, 16 * (low // 4 % 2) + 4 * (low % 4) + a // 4


def filter_detector(
    load, template_ref, near_ref, mix_ref, table_ref, digit_ref, fold_ref, out_ref, base, work_ref, last_ref
):
    lower = low_lanes((8, 128))

    def spread(low, carry):
        values = []
        for a in range(8):
            one = load(*slot_of(a, low))
            two = load(*slot_of(a + 8, low))
            add, sub = one + two, one - two
            re, im = jnp.where(lower, add, swap(sub)), jnp.where(lower, swap(add), sub)
            cosine, sine = fold_ref[a, 0:1, :], fold_ref[a, 1:2, :]
            values.append((re * cosine - im * sine, re * sine + im * cosine) if a else (re, im))
        for pair, (re, im) in enumerate(butterfly(values, -1)):
            cosine, sine = digit_ref[pair, 0, tile_rows(8 * low), :], digit_ref[pair, 1, tile_rows(8 * low), :]
            lanes = slice(128 * (pair % 2), 128 * (pair % 2) + 128)
            work_ref[pair // 2, tile_rows(8 * low), lanes] = re * cosine + im * sine
            work_ref[pair // 2, tile_rows(128 + 8 * low), lanes] = im * cosine - re * sine
        return carry

    lax.fori_loop(0, 16, spread, 0)

    for quad in range(4):
        high, low = halves(work_ref[quad])
        spectrum = dot(table_ref[0, 0], high) + dot(table_ref[0, 0], low) + dot(table_ref[0, 1], high)
        s_re, s_im = spectrum[0:128], spectrum[128:256]
        rows = [pl.ds(4 * quad + 2 * k, 128, stride=16) for k in range(2)]
        h_re = jnp.concatenate([template_ref[0, r, :] for r in rows], axis=1)
        h_im = jnp.concatenate([template_ref[1, r, :] for r in rows], axis=1)
        product = jnp.concatenate((s_re * h_re + s_im * h_im, s_im * h_re - s_re * h_im), axis=0)
        high, low = halves(product)
        series = dot(table_ref[1, 0], high) + dot(table_ref[1, 0], low) + dot(table_ref[1, 1], high)
        for k in range(2):
            lanes = slice(128 * k, 128 * k + 128)
            re, im = series[0:128, lanes], series[128:256, lanes]
            cosine, sine = digit_ref[2 * quad + k, 0], digit_ref[2 * quad + k, 1]
            re, im = re * cosine - im * sine, re * sine + im * cosine
            cosine, sine = near_ref[0], near_ref[1]
            work_ref[quad, 0:128, lanes] = re * cosine - im * sine
            work_ref[quad, 128:256, lanes] = re * sine + im * cosine

    def collect(step, carry):
        values = []
        for pair in range(8):
            lanes = slice(128 * (pair % 2), 128 * (pair % 2) + 128)
            rows = tile_rows(8 * step), tile_rows(128 + 8 * step)
            values.append((work_ref[pair // 2, rows[0], lanes], work_ref[pair // 2, rows[1], lanes]))
        for k, (re, im) in enumerate(butterfly(values, 1)):
            last_ref[k, tile_rows(8 * step), 0:128] = re
            last_ref[k, tile_rows(8 * step), 128:256] = im
        return carry

    lax.fori_loop(0, 16, collect, 0)
    for k in range(8):
        high, low = halves(last_ref[k])
        mixed = dot(high, mix_ref[0, k]) + dot(low, mix_ref[0, k]) + dot(high, mix_ref[1, k])
        for quarter in range(4):
            rows = slice(32 * quarter, 32 * quarter + 32)
            out_ref[4 * k + quarter, base:base + 32, :] = mixed[rows, 0:128]
            out_ref[4 * k + quarter, base + 32:base + 64, :] = mixed[rows, 128:256]


def filter_first(member_ref, *refs):
    pieces, tables, norm_ref = refs[:8], refs[8:14], refs[14]
    out_ref, work_ref, last_ref, held_ref, sems = refs[15:]
    side, core = member_ref[0], member_ref[1]
    copies = []
    for at, piece in enumerate(pieces):
        slot = 2 * lax.rem(side + (4 - at % 4), 4) + (core if at < 4 else 1 - core)
        copy = pltpu.make_async_copy(piece, held_ref.at[slot], sems.at[at])
        copy.start()
        copies.append(copy)
    for rank in range(RANKS):
        out_ref[rank, 64:72, :] = norm_ref[...]
    for copy in copies:
        copy.wait()
    filter_detector(lambda member, rank: held_ref[member, rank], *tables, out_ref, 0, work_ref, last_ref)


def filter_rest(in_ref, *refs):
    tables, (out_ref, work_ref, last_ref) = refs[:6], refs[6:]
    for at in range(2):
        filter_detector(
            lambda member, rank, rows=slice(8 * at, 8 * at + 8): in_ref[member, rank, rows, :],
            *tables, out_ref, 64 * at, work_ref, last_ref,
        )


def detector_power(in_ref, base, twiddle_ref, wide_ref, work_ref):
    def step_fn(step, carry):
        values = [
            (in_ref[r, tile_rows(base + 8 * step), :], in_ref[r, tile_rows(base + 32 + 8 * step), :])
            for r in range(RANKS)
        ]
        for digit, (re, im) in enumerate(butterfly(values, 1)):
            cosine, sine = twiddle_ref[0, digit:digit + 1, :], twiddle_ref[1, digit:digit + 1, :]
            at = 16 * (digit // 16) + 4 * (digit % 4) + digit // 4 % 4
            rows = tile_rows(32 * at + 8 * step)
            work_ref[rows, 0:128] = re * cosine - im * sine
            work_ref[rows, 128:256] = im * cosine + re * sine
        return carry

    lax.fori_loop(0, 4, step_fn, 0)

    def power_of(quad):
        high, low = halves(work_ref[pl.ds(pl.multiple_of(128 * quad, 128), 128), :])
        full = dot(high, wide_ref[0]) + dot(low, wide_ref[0]) + dot(high, wide_ref[1])
        re, im = full[:, 0:128], full[:, 128:256]
        return re * re + im * im

    return power_of


def start_power(in_ref, twiddle_ref, wide_ref, out_ref, norm_ref, work_ref):
    total = jnp.zeros((8, 128), F32)
    for rank in range(RANKS):
        total = total + in_ref[rank, 64:72, :]
    norm_ref[...] = total
    power_of = detector_power(in_ref, 0, twiddle_ref, wide_ref, work_ref)

    def step_fn(quad, carry):
        out_ref[pl.ds(pl.multiple_of(128 * quad, 128), 128), :] = power_of(quad)
        return carry

    lax.fori_loop(0, 8, step_fn, 0)


def finish_power(in_ref, twiddle_ref, wide_ref, sum_ref, norm_ref, out_ref, one_ref, two_ref):
    first = detector_power(in_ref, 0, twiddle_ref, wide_ref, one_ref)
    second = detector_power(in_ref, 64, twiddle_ref, wide_ref, two_ref)
    scale = 1.0 / (FULL * (jnp.sum(norm_ref[...]) + EPSILON))
    for quad in range(8):
        rows = slice(128 * quad, 128 * quad + 128)
        turned = ((first(quad) + second(quad) + sum_ref[rows, :]) * scale).T
        for g in range(8):
            start = 32 * (quad // 4) + 4 * (quad % 4) + 16 * (g // 4) + g % 4
            out_ref[pl.ds(start, 16, stride=64), :] = turned[16 * g:16 * g + 16, :]


def best_template(*refs):
    refs[4][...] = jnp.maximum(jnp.maximum(refs[0][...], refs[1][...]), jnp.maximum(refs[2][...], refs[3][...]))


def merge_templates(side_ref, *refs):
    one_ref, two_ref, out_ref = refs[4:]
    for block in range(8):
        rows = slice(32 * block, 32 * block + 32)
        best = jnp.maximum(one_ref[rows, :], two_ref[rows, :])
        for step in range(4):
            t = lax.rem(side_ref[0] + (4 - step), 4)
            out_ref[4 * block + t, 0:32, :] = refs[step][rows, :]
            out_ref[4 * block + t, 32:64, :] = best


def place_samples(in_ref, out_ref, best_ref):
    for k in range(8):
        for first, target in ((0, out_ref), (32, best_ref)):
            parts = [in_ref[4 * k + quarter, first:first + 32, :] for quarter in range(4)]
            for u in range(4):
                joined = jnp.concatenate([p[:, 32 * u:32 * u + 32] for p in parts], axis=1)
                for h in range(2):
                    target[pl.ds(256 * u + 8 * h + k, 16, stride=16), :] = joined[16 * h:16 * h + 16]


PARAMS = pltpu.CompilerParams(vmem_limit_bytes=VMEM_LIMIT)


def shape(*dims):
    return jax.ShapeDtypeStruct(dims, F32)


def call(kernel, out, specs, scratch=(), **kwargs):
    many = isinstance(out, (tuple, list))
    whole = pl.BlockSpec(memory_space=pltpu.VMEM)
    return pl.pallas_call(
        kernel,
        out_shape=out,
        in_specs=specs,
        out_specs=[whole] * len(out) if many else whole,
        scratch_shapes=list(scratch),
        compiler_params=PARAMS,
        **kwargs,
    )


def cost(us):
    return pl.CostEstimate(flops=int(us * 1e9), bytes_accessed=int(us * 1e6), transcendentals=0)


TIME = ("zp", "zl", "x")
BINS = ("zl", "x", "y")
ACROSS = [(0, 1), (1, 0)]


def forward(value, axis, step):
    return lax.ppermute(value, axis, [(i, (i + step) % 4) for i in range(4)]) if step else value


def gather_pieces(value, ready):
    own = [value] + [forward(value, "zp", step) for step in (1, 2, 3)]
    own, ready = lax.optimization_barrier((own, ready))
    return own + [lax.ppermute(one, "core", ACROSS) for one in own], ready


def spread_templates(masked, y):
    pieces = [lax.dynamic_index_in_dim(masked, y, 0, False)]
    for step in (1, 2, 3):
        pieces.append(forward(lax.dynamic_index_in_dim(masked, (y + step) % 4, 0, False), "y", step))
    return jnp.stack(pieces)


def move_templates(pieces, y, side, step):
    return forward(lax.dynamic_index_in_dim(pieces, (y - side - step) % 4, 0, False), "zp", step)


def local(strain, templates, pattern, cutoff):
    side, low, x, y, core = (lax.axis_index(n).astype(jnp.int32) for n in ("zp", "zl", "x", "y", "core"))
    me, group, place = 8 * side + 4 * low + x, 2 * y + core, 16 * low + 4 * x + y
    vmem = pl.BlockSpec(memory_space=pltpu.VMEM)
    smem = pl.BlockSpec(memory_space=pltpu.SMEM)
    anywhere = pl.BlockSpec(memory_space=pl.ANY)

    samples = strain.reshape(2, 3, 64, 16, 128).transpose(1, 2, 3, 0, 4).reshape(192, 32, 128)
    columns = pl.pallas_call(
        lambda group_ref, strain_ref, out_ref: gather_columns(group_ref, strain_ref.reshape(1536, 128), out_ref),
        out_shape=shape(RANKS, 24, 128),
        grid_spec=pltpu.PrefetchScalarGridSpec(
            num_scalar_prefetch=1,
            grid=(1,),
            in_specs=[pl.BlockSpec((192, 8, 128), lambda i, at: (0, at[0] // 2, 0))],
            out_specs=pl.BlockSpec((RANKS, 24, 128), lambda i, at: (0, 0, 0)),
        ),
        compiler_params=PARAMS,
        cost_estimate=cost(3),
    )(group.reshape(1), samples)
    columns = lax.all_to_all(columns, TIME, 0, 0, tiled=True)

    block_index = jnp.arange(pattern.shape[1], dtype=jnp.int32)
    active = pattern.astype(F32) * (block_index[None, :] < cutoff[:, None]).astype(F32)
    weight = jnp.repeat(active, SIDE // pattern.shape[1], axis=1)
    masked = jnp.swapaxes(templates.reshape(2, 4, 16, SIDE), 0, 1) * weight
    pieces = spread_templates(masked, y)
    pieces, group, me, place = lax.optimization_barrier((pieces, group, me, place))
    moved = [move_templates(pieces, y, side, step) for step in (0, 1, 2, 3)]

    row = jnp.arange(256, dtype=jnp.int32)[:, None]
    lane = jnp.arange(128, dtype=jnp.int32)[None, :]
    first_phase = phases((256 * group + 8 * me + row % 8) * (row // 8 + 32 * (lane % 64)), -1.0)
    columns, first_phase = lax.optimization_barrier((columns, first_phase))

    def first_bins(columns):
        rows = call(
            first_section,
            shape(RANKS * 24, 128),
            [vmem] * 5,
            [pltpu.VMEM((256, 256), F32), pltpu.VMEM((256, 128), F32), pltpu.VMEM((3, 256, 128), F32)],
            cost_estimate=cost(4),
        )(columns, jnp.asarray(row_twiddle()), jnp.asarray(first_table(2)), jnp.asarray(first_table(1)), first_phase)
        return lax.all_to_all(rows.reshape(RANKS, 24, 128), BINS, 0, 0, tiled=True)

    rows = lax.cond(place >= 0, first_bins, lambda columns: columns, columns)
    rows, moved, place = lax.optimization_barrier((rows, moved, place))
    near = phases(jnp.arange(128, dtype=jnp.int32)[:, None] * (512 * (lane // 16 % 4) + 16 * place + lane % 16), 1.0)
    mix = mixing_tables(place)
    bank, norm = call(
        prepare_templates,
        (shape(2, SIDE, 128), shape(8, 128)),
        [smem] + [anywhere] * 4,
        [pltpu.VMEM((4, 2, 16, SIDE), F32), pltpu.SemaphoreType.DMA((4,))],
        cost_estimate=cost(4),
    )(side.reshape(1), *moved)

    tables = [jnp.asarray(t) for t in (column_table(), digit_twiddle(), fold_twiddle())]
    others = lax.all_gather(rows[:, 0:16, :], ("zp", "core"), axis=0)
    pieces, (bank, near, mix) = gather_pieces(rows[:, 16:24, :], (bank, near, mix))
    tables = [near, mix] + tables
    work = [pltpu.VMEM((4, 256, 256), F32), pltpu.VMEM((8, 128, 256), F32)]
    first = call(
        filter_first,
        shape(RANKS, 72, 128),
        [smem] + [anywhere] * 8 + [vmem] * 7,
        work + [pltpu.VMEM((GROUPS, RANKS, 8, 128), F32), pltpu.SemaphoreType.DMA((8,))],
        cost_estimate=cost(8),
    )(jnp.stack((side, core)), *pieces, bank, *tables, norm)
    first = lax.all_to_all(first, BINS, 0, 0, tiled=True)
    second = call(
        filter_rest, shape(RANKS, 128, 128), [vmem] * 7, work, cost_estimate=cost(12)
    )(others, bank, *tables)
    second = lax.all_to_all(second, BINS, 0, 0, tiled=True)

    twiddle, wide = jnp.asarray(inner_twiddle()), jnp.asarray(last_table())
    work = pltpu.VMEM((1024, 256), F32)
    total, whole_norm = call(
        start_power, (shape(1024, 128), shape(8, 128)), [vmem] * 3, [work], cost_estimate=cost(3)
    )(first, twiddle, wide)
    power = call(finish_power, shape(1024, 128), [vmem] * 5, [work] * 2, cost_estimate=cost(6))(
        second, twiddle, wide, total, whole_norm
    )
    power = power.reshape(4, 256, 128)
    power = [forward(lax.dynamic_index_in_dim(power, (side + step) % 4, 0, False), "zp", step) for step in range(4)]
    best = call(best_template, shape(256, 128), [vmem] * 4, cost_estimate=cost(1))(*power)
    other = lax.ppermute(best, "core", ACROSS)
    power = call(merge_templates, shape(RANKS, 64, 128), [smem] + [vmem] * 6, cost_estimate=cost(2))(
        side.reshape(1), *power, best, other
    )
    power = lax.all_to_all(power, BINS, 0, 0, tiled=True)
    snr, peak = call(place_samples, (shape(1024, 128), shape(1024, 128)), [vmem], cost_estimate=cost(2))(power)
    return snr.reshape(1, 64 * SIDE), peak.reshape(64 * SIDE)


def solution(mesh):
    mesh = jax.sharding.Mesh(mesh.devices.reshape(4, 2, 4, 4, 2), ("zp", "zl", "x", "y", "core"))
    group = ("y", "core")
    in_specs = (P(None, None, TIME), P(None, group, TIME, None), P(group, None), P(group))
    out_specs = (P(group, TIME), P(TIME))
    return jax.shard_map(local, mesh=mesh, in_specs=in_specs, out_specs=out_specs, check_vma=False)
```

```python
import functools
import math

import jax
import jax.numpy as jnp
import numpy as np
from jax import lax
from jax.experimental import pallas as pl
from jax.experimental.pallas import tpu as pltpu
from jax.sharding import PartitionSpec as P

EPSILON = 1e-06
SIDE = 2048
FULL = SIDE * SIDE
DETECTORS = 3
RANKS = 32
GROUPS = 8
F32 = jnp.float32
BF16 = jnp.bfloat16
VMEM_LIMIT = 24 * 1024 * 1024


def split_table(table):
    high = table.astype(np.float32).astype(jnp.bfloat16)
    low = (table - high.astype(np.float64)).astype(np.float32).astype(jnp.bfloat16)
    return np.stack((high, low))


def first_table(copies):
    theta = 2.0 * np.pi * np.outer(np.arange(64), np.arange(64)) / 64.0
    eye = np.eye(copies)
    cosine, sine = np.kron(eye, np.cos(theta)), np.kron(eye, np.sin(theta))
    return split_table(np.block([[cosine, -sine], [sine, cosine]]))


def last_table():
    theta = 2.0 * np.pi * np.outer(np.arange(16), np.arange(16)) / 16.0
    eye = np.eye(8)
    cosine, sine = np.kron(eye, np.cos(theta)), np.kron(eye, np.sin(theta))
    return split_table(np.block([[cosine, sine], [-sine, cosine]]))


def column_table():
    theta = 2.0 * np.pi * np.outer(np.arange(128), np.arange(128)) / 128.0
    cosine, sine = np.cos(theta), np.sin(theta)
    whole = np.block([[cosine, sine], [-sine, cosine]])
    return np.stack((split_table(whole), split_table(whole.T)))


def digit_twiddle():
    digit = 2 * np.arange(8)[:, None, None] + (np.arange(128) // 64)[None, None, :]
    theta = 2.0 * np.pi * (np.arange(128)[None, :, None] * digit) / SIDE
    return np.stack((np.cos(theta), np.sin(theta)), axis=1).astype(np.float32)


def fold_twiddle():
    theta = 2.0 * np.pi * np.outer(np.arange(8), np.arange(128) // 64) / 16.0
    return np.stack((np.cos(theta), -np.sin(theta)), axis=1).astype(np.float32)


def row_twiddle():
    theta = 2.0 * np.pi * np.outer(np.arange(32), np.arange(128) % 64) / SIDE
    return np.stack((np.cos(theta), np.sin(theta))).astype(np.float32)


def inner_twiddle():
    theta = 2.0 * np.pi * np.outer(np.arange(32), np.arange(128) % 16) / 512.0
    return np.stack((np.cos(theta), np.sin(theta))).astype(np.float32)


def phases(turns, orient):
    angle = (turns % FULL).astype(F32) * (orient * 2.0 * math.pi / FULL)
    return jnp.stack((jnp.cos(angle), jnp.sin(angle)))


def mixing_tables(place):
    k = jnp.arange(8, dtype=jnp.int32)[:, None, None]
    into = jnp.arange(128, dtype=jnp.int32)[None, :, None]
    out = jnp.arange(128, dtype=jnp.int32)[None, None, :]
    block, w = k + 8 * (out // 64), out // 16 % 4
    e, a, i = into // 64, into // 16 % 4, into % 16
    turns = e * block * (FULL // 16) + 128 * block * (512 * a + 16 * place + i)
    turns = turns % FULL + a * w * (FULL // 4) + (16 * place + i) * w * SIDE
    cosine, sine = phases(turns, 1.0) * (i == out % 16).astype(F32)
    whole = jnp.concatenate(
        (jnp.concatenate((cosine, sine), axis=2), jnp.concatenate((-sine, cosine), axis=2)), axis=1
    )
    high = lax.reduce_precision(whole, 8, 7)
    return jnp.stack((high.astype(BF16), (whole - high).astype(BF16)))


def times_unit(value, numer, denom, orient):
    re, im = value
    numer = numer % denom
    if numer == 0:
        return value
    if 8 * numer % denom == 0:
        eighth = 8 * numer // denom
        if eighth == 4:
            return -re, -im
        if eighth in (2, 6):
            return (-im, re) if (eighth == 2) == (orient > 0) else (im, -re)
    cosine = math.cos(2.0 * math.pi * numer / denom)
    sine = orient * math.sin(2.0 * math.pi * numer / denom)
    return re * cosine - im * sine, re * sine + im * cosine


def butterfly(values, orient):
    count = len(values)
    if count == 1:
        return values
    if count == 2:
        (ar, ai), (br, bi) = values
        return [(ar + br, ai + bi), (ar - br, ai - bi)]
    if count == 4:
        (ar, ai), (br, bi), (cr, ci), (dr, di) = values
        sr, si, tr, ti = ar + cr, ai + ci, ar - cr, ai - ci
        ur, ui, vr, vi = br + dr, bi + di, br - dr, bi - di
        if orient > 0:
            return [(sr + ur, si + ui), (tr - vi, ti + vr), (sr - ur, si - ui), (tr + vi, ti - vr)]
        return [(sr + ur, si + ui), (tr + vi, ti - vr), (sr - ur, si - ui), (tr - vi, ti + vr)]
    radix = 4 if count % 4 == 0 else 2
    inner = count // radix
    parts = [butterfly(values[s::radix], orient) for s in range(radix)]
    out = [None] * count
    for k in range(inner):
        joined = butterfly([times_unit(parts[s][k], s * k, count, orient) for s in range(radix)], orient)
        for part in range(radix):
            out[k + inner * part] = joined[part]
    return out


def halves(value):
    high = value.astype(BF16)
    return high, (value - high.astype(F32)).astype(BF16)


def dot(a, b, contract=((1,), (0,))):
    return lax.dot_general(a, b, (contract, ((), ())), preferred_element_type=F32)


def low_lanes(shape):
    return lax.broadcasted_iota(jnp.int32, shape, 1) < 64


def swap(value):
    return pltpu.roll(value, 64, 1)


def fetch(pairs, sems):
    copies = [pltpu.make_async_copy(source, target, sems.at[at]) for at, (source, target) in enumerate(pairs)]
    for copy in copies:
        copy.start()
    return copies


def tile_rows(start):
    return pl.ds(pl.multiple_of(start, 8), 8)


def gather_columns(group_ref, strain_ref, out_ref):
    first = 4 * lax.rem(group_ref[0], 2)

    def piece(detector, tile, part):
        return strain_ref[pl.ds(512 * detector + first + 2 * tile + part, 64, stride=8), :]

    for tile in range(2):
        for at, (one, two) in enumerate((((0, 0), (1, 0)), ((0, 1), (1, 1)), ((2, 0), (2, 1)))):
            joined = jnp.concatenate((piece(one[0], tile, one[1]), piece(two[0], tile, two[1])), axis=0)
            out_ref[16 * tile:16 * tile + 16, 8 * at:8 * at + 8, :] = joined.T.reshape(16, 8, 128)


def prepare_templates(side_ref, *refs):
    pieces, (out_ref, norm_ref, held_ref, sems) = refs[:4], refs[4:]
    copies = []
    for at, piece in enumerate(pieces):
        copy = pltpu.make_async_copy(piece, held_ref.at[lax.rem(side_ref[0] + (4 - at), 4)], sems.at[at])
        copy.start()
        copies.append(copy)
    for copy in copies:
        copy.wait()
    total = jnp.zeros((64, 128), F32)
    for chunk in range(16):
        lanes = slice(128 * chunk, 128 * chunk + 128)
        for part in range(2):
            value = jnp.concatenate([held_ref[a, part, :, lanes] for a in range(4)], axis=0)
            total = total + value * value
            out_ref[part, lanes, :] = jnp.concatenate((value, pltpu.roll(value, 127, 1)), axis=0).T
    norm_ref[...] = jnp.sum(total.reshape(8, 8, 128), axis=0)


def first_section(in_ref, twiddle_ref, wide_ref, narrow_ref, phase_ref, out_ref, pair_ref, single_ref, turn_ref):
    lower = low_lanes((8, 128))
    for at in range(2):
        values = []
        for rank in range(RANKS):
            if at == 0:
                values.append((in_ref[rank, 0:8, :], in_ref[rank, 8:16, :]))
            else:
                one = in_ref[rank, 16:24, :]
                values.append((one, swap(one)))
        for digit, (re, im) in enumerate(butterfly(values, -1)):
            cosine, sine = twiddle_ref[0, digit:digit + 1, :], twiddle_ref[1, digit:digit + 1, :]
            re, im = re * cosine + im * sine, im * cosine - re * sine
            rows = slice(8 * digit, 8 * digit + 8)
            if at == 0:
                pair_ref[rows, 0:128] = re
                pair_ref[rows, 128:256] = im
            else:
                single_ref[rows, :] = jnp.where(lower, re, swap(im))
    high, low = halves(pair_ref[...])
    pair = dot(high, wide_ref[0]) + dot(low, wide_ref[0]) + dot(high, wide_ref[1])
    high, low = halves(single_ref[...])
    single = dot(high, narrow_ref[0]) + dot(low, narrow_ref[0]) + dot(high, narrow_ref[1])
    cosine, sine = phase_ref[0], phase_ref[1]
    re, im = pair[:, 0:128], pair[:, 128:256]
    turn_ref[0] = re * cosine - im * sine
    turn_ref[1] = im * cosine + re * sine
    turn_ref[2] = single * cosine + swap(single) * jnp.where(low_lanes((256, 128)), -sine, sine)
    for at in range(DETECTORS):
        for quad in range(2):
            blocks = []
            for part in range(2):
                source, start = (part, 64 * at) if at < 2 else (2, 64 * part)
                cols = [turn_ref[source, pl.ds(4 * quad + u, 32, stride=8), :] for u in range(4)]
                for a in range(4):
                    lanes = slice(start + 16 * a, start + 16 * a + 16)
                    blocks.append(jnp.concatenate([c[16 * h:16 * h + 16, lanes] for c in cols for h in range(2)], axis=1))
            turned = jnp.concatenate(blocks, axis=0).T
            for u in range(4):
                for h in range(2):
                    rows = pl.ds(24 * h + 8 * at + 4 * quad + u, 16, stride=48)
                    out_ref[rows, :] = turned[32 * u + 16 * h:32 * u + 16 * h + 16, :]


def slot_of(a, low):
    return 4 * (a % 2) + 2 * (low // 8) + a // 2 % 2, 16 * (low // 4 % 2) + 4 * (low % 4) + a // 4


def filter_detector(
    load, template_ref, near_ref, mix_ref, table_ref, digit_ref, fold_ref, out_ref, base, work_ref, last_ref, waits
):
    lower = low_lanes((8, 128))

    def spread(low, carry):
        values = []
        for a in range(8):
            one = load(*slot_of(a, low))
            two = load(*slot_of(a + 8, low))
            add, sub = one + two, one - two
            re, im = jnp.where(lower, add, swap(sub)), jnp.where(lower, swap(add), sub)
            cosine, sine = fold_ref[a, 0:1, :], fold_ref[a, 1:2, :]
            values.append((re * cosine - im * sine, re * sine + im * cosine) if a else (re, im))
        for pair, (re, im) in enumerate(butterfly(values, -1)):
            cosine, sine = digit_ref[pair, 0, tile_rows(8 * low), :], digit_ref[pair, 1, tile_rows(8 * low), :]
            lanes = slice(128 * (pair % 2), 128 * (pair % 2) + 128)
            work_ref[pair // 2, tile_rows(8 * low), lanes] = re * cosine + im * sine
            work_ref[pair // 2, tile_rows(128 + 8 * low), lanes] = im * cosine - re * sine
        return carry

    lax.fori_loop(0, 16, spread, 0, unroll=2)
    for copy in waits[0]:
        copy.wait()

    for quad in range(4):
        high, low = halves(work_ref[quad])
        spectrum = dot(table_ref[0, 0], high) + dot(table_ref[0, 0], low) + dot(table_ref[0, 1], high)
        s_re, s_im = spectrum[0:128], spectrum[128:256]
        rows = [pl.ds(4 * quad + 2 * k, 128, stride=16) for k in range(2)]
        h_re = jnp.concatenate([template_ref[0, r, :] for r in rows], axis=1)
        h_im = jnp.concatenate([template_ref[1, r, :] for r in rows], axis=1)
        product = jnp.concatenate((s_re * h_re + s_im * h_im, s_im * h_re - s_re * h_im), axis=0)
        high, low = halves(product)
        series = dot(table_ref[1, 0], high) + dot(table_ref[1, 0], low) + dot(table_ref[1, 1], high)
        for k in range(2):
            lanes = slice(128 * k, 128 * k + 128)
            re, im = series[0:128, lanes], series[128:256, lanes]
            cosine, sine = digit_ref[2 * quad + k, 0], digit_ref[2 * quad + k, 1]
            re, im = re * cosine - im * sine, re * sine + im * cosine
            cosine, sine = near_ref[0], near_ref[1]
            work_ref[quad, 0:128, lanes] = re * cosine - im * sine
            work_ref[quad, 128:256, lanes] = re * sine + im * cosine

    def collect(step, carry):
        values = []
        for pair in range(8):
            lanes = slice(128 * (pair % 2), 128 * (pair % 2) + 128)
            rows = tile_rows(8 * step), tile_rows(128 + 8 * step)
            values.append((work_ref[pair // 2, rows[0], lanes], work_ref[pair // 2, rows[1], lanes]))
        for k, (re, im) in enumerate(butterfly(values, 1)):
            last_ref[k, tile_rows(8 * step), 0:128] = re
            last_ref[k, tile_rows(8 * step), 128:256] = im
        return carry

    lax.fori_loop(0, 16, collect, 0, unroll=2)
    for copy in waits[1]:
        copy.wait()
    for k in range(8):
        high, low = halves(last_ref[k])
        mixed = dot(high, mix_ref[0, k]) + dot(low, mix_ref[0, k]) + dot(high, mix_ref[1, k])
        for quarter in range(4):
            rows = slice(32 * quarter, 32 * quarter + 32)
            out_ref[4 * k + quarter, base:base + 32, :] = mixed[rows, 0:128]
            out_ref[4 * k + quarter, base + 32:base + 64, :] = mixed[rows, 128:256]


def filter_first(member_ref, *refs):
    pieces, mix_hbm, tables, norm_ref = refs[:8], refs[8], refs[9:14], refs[14]
    out_ref, work_ref, last_ref, mix_ref, held_ref, sems = refs[15:]
    side, core = member_ref[0], member_ref[1]
    pairs = []
    for at, piece in enumerate(pieces):
        slot = 2 * lax.rem(side + (4 - at % 4), 4) + (core if at < 4 else 1 - core)
        pairs.append((piece, held_ref.at[slot]))
    copies = fetch(pairs + [(mix_hbm, mix_ref)], sems)
    for rank in range(RANKS):
        out_ref[rank, 64:72, :] = norm_ref[...]
    for copy in copies[:8]:
        copy.wait()
    bank_ref, near_ref, table_ref, digit_ref, fold_ref = tables
    filter_detector(
        lambda member, rank: held_ref[member, rank],
        bank_ref, near_ref, mix_ref, table_ref, digit_ref, fold_ref, out_ref, 0, work_ref, last_ref, ((), copies[8:]),
    )


def filter_rest(in_hbm, bank_hbm, near_hbm, mix_hbm, table_hbm, digit_hbm, fold_hbm, out_ref, *scratch):
    work_ref, last_ref, bank_ref, near_ref, mix_ref, table_ref, digit_ref, fold_ref, held_ref, sems = scratch
    pairs = [(in_hbm.at[:, :, 8 * at:8 * at + 8, :], held_ref.at[at]) for at in range(2)]
    pairs = [pairs[0], (fold_hbm, fold_ref), (digit_hbm, digit_ref), (table_hbm, table_ref), (bank_hbm, bank_ref)] + [
        (near_hbm, near_ref), (mix_hbm, mix_ref), pairs[1]
    ]
    copies = fetch(pairs, sems)
    for copy in copies[:3]:
        copy.wait()
    for at in range(2):
        filter_detector(
            lambda member, rank, at=at: held_ref[at, member, rank],
            bank_ref, near_ref, mix_ref, table_ref, digit_ref, fold_ref, out_ref, 64 * at, work_ref, last_ref,
            ((), ()) if at else (copies[3:6], copies[6:8]),
        )


def detector_power(in_ref, base, twiddle_ref, wide_ref, work_ref):
    def step_fn(step, carry):
        values = [
            (in_ref[r, tile_rows(base + 8 * step), :], in_ref[r, tile_rows(base + 32 + 8 * step), :])
            for r in range(RANKS)
        ]
        for digit, (re, im) in enumerate(butterfly(values, 1)):
            cosine, sine = twiddle_ref[0, digit:digit + 1, :], twiddle_ref[1, digit:digit + 1, :]
            at = 16 * (digit // 16) + 4 * (digit % 4) + digit // 4 % 4
            rows = tile_rows(32 * at + 8 * step)
            work_ref[rows, 0:128] = re * cosine - im * sine
            work_ref[rows, 128:256] = im * cosine + re * sine
        return carry

    lax.fori_loop(0, 4, step_fn, 0)

    def power_of(quad):
        high, low = halves(work_ref[pl.ds(pl.multiple_of(128 * quad, 128), 128), :])
        full = dot(high, wide_ref[0]) + dot(low, wide_ref[0]) + dot(high, wide_ref[1])
        re, im = full[:, 0:128], full[:, 128:256]
        return re * re + im * im

    return power_of


def start_power(in_ref, twiddle_ref, wide_ref, out_ref, work_ref):
    total = jnp.zeros((8, 128), F32)
    for rank in range(RANKS):
        total = total + in_ref[rank, 64:72, :]
    out_ref[1024:1032, :] = total
    out_ref[1032:1096, :] = twiddle_ref[...].reshape(64, 128)
    power_of = detector_power(in_ref, 0, twiddle_ref, wide_ref, work_ref)

    def step_fn(quad, carry):
        out_ref[pl.ds(pl.multiple_of(128 * quad, 128), 128), :] = power_of(quad)
        return carry

    lax.fori_loop(0, 8, step_fn, 0)


def finish_power(in_ref, wide_ref, sum_ref, out_ref, one_ref, two_ref):
    twiddle_ref = sum_ref.at[1032:1096].reshape(2, 32, 128)
    first = detector_power(in_ref, 0, twiddle_ref, wide_ref, one_ref)
    second = detector_power(in_ref, 64, twiddle_ref, wide_ref, two_ref)
    scale = 1.0 / (FULL * (jnp.sum(sum_ref[1024:1032, :]) + EPSILON))
    for quad in range(8):
        rows = slice(128 * quad, 128 * quad + 128)
        turned = ((first(quad) + second(quad) + sum_ref[rows, :]) * scale).T
        for g in range(8):
            start = 32 * (quad // 4) + 4 * (quad % 4) + 16 * (g // 4) + g % 4
            out_ref[pl.ds(start, 16, stride=64), :] = turned[16 * g:16 * g + 16, :]


def best_template(*refs):
    refs[4][...] = jnp.maximum(jnp.maximum(refs[0][...], refs[1][...]), jnp.maximum(refs[2][...], refs[3][...]))


def merge_templates(side_ref, *refs):
    one_ref, two_ref, out_ref = refs[4:]
    for block in range(8):
        rows = slice(32 * block, 32 * block + 32)
        best = jnp.maximum(one_ref[rows, :], two_ref[rows, :])
        for step in range(4):
            t = lax.rem(side_ref[0] + (4 - step), 4)
            out_ref[4 * block + t, 0:32, :] = refs[step][rows, :]
            out_ref[4 * block + t, 32:64, :] = best


def place_samples(in_ref, out_ref, best_ref):
    for k in range(8):
        for first, target in ((0, out_ref), (32, best_ref)):
            parts = [in_ref[4 * k + quarter, first:first + 32, :] for quarter in range(4)]
            for u in range(4):
                joined = jnp.concatenate([p[:, 32 * u:32 * u + 32] for p in parts], axis=1)
                for h in range(2):
                    target[pl.ds(256 * u + 8 * h + k, 16, stride=16), :] = joined[16 * h:16 * h + 16]


PARAMS = pltpu.CompilerParams(vmem_limit_bytes=VMEM_LIMIT)


def shape(*dims):
    return jax.ShapeDtypeStruct(dims, F32)


def call(kernel, out, specs, scratch=(), limit=VMEM_LIMIT, **kwargs):
    many = isinstance(out, (tuple, list))
    whole = pl.BlockSpec(memory_space=pltpu.VMEM)
    return pl.pallas_call(
        kernel,
        out_shape=out,
        in_specs=specs,
        out_specs=[whole] * len(out) if many else whole,
        scratch_shapes=list(scratch),
        compiler_params=pltpu.CompilerParams(vmem_limit_bytes=limit),
        **kwargs,
    )


def cost(us):
    return pl.CostEstimate(flops=int(us * 1e9), bytes_accessed=int(us * 1e6), transcendentals=0)


TIME = ("zp", "zl", "x")
BINS = ("zl", "x", "y")
ACROSS = [(0, 1), (1, 0)]


def forward(value, axis, step):
    return lax.ppermute(value, axis, [(i, (i + step) % 4) for i in range(4)]) if step else value


def gather_pieces(value, ready):
    own = [value] + [forward(value, "zp", step) for step in (1, 2, 3)]
    own, ready = lax.optimization_barrier((own, ready))
    return own + [lax.ppermute(one, "core", ACROSS) for one in own], ready


def spread_templates(masked, y):
    pieces = [lax.dynamic_index_in_dim(masked, y, 0, False)]
    for step in (1, 2, 3):
        pieces.append(forward(lax.dynamic_index_in_dim(masked, (y + step) % 4, 0, False), "y", step))
    return jnp.stack(pieces)


def move_templates(pieces, y, side, step):
    return forward(lax.dynamic_index_in_dim(pieces, (y - side - step) % 4, 0, False), "zp", step)


def local(strain, templates, pattern, cutoff):
    side, low, x, y, core = (lax.axis_index(n).astype(jnp.int32) for n in ("zp", "zl", "x", "y", "core"))
    me, group, place = 8 * side + 4 * low + x, 2 * y + core, 16 * low + 4 * x + y
    vmem = pl.BlockSpec(memory_space=pltpu.VMEM)
    smem = pl.BlockSpec(memory_space=pltpu.SMEM)
    anywhere = pl.BlockSpec(memory_space=pl.ANY)

    samples = strain.reshape(2, 3, 64, 16, 128).transpose(1, 2, 3, 0, 4).reshape(192, 32, 128)
    columns = pl.pallas_call(
        lambda group_ref, strain_ref, out_ref: gather_columns(group_ref, strain_ref.reshape(1536, 128), out_ref),
        out_shape=shape(RANKS, 24, 128),
        grid_spec=pltpu.PrefetchScalarGridSpec(
            num_scalar_prefetch=1,
            grid=(1,),
            in_specs=[pl.BlockSpec((192, 8, 128), lambda i, at: (0, at[0] // 2, 0))],
            out_specs=pl.BlockSpec((RANKS, 24, 128), lambda i, at: (0, 0, 0)),
        ),
        compiler_params=PARAMS,
        cost_estimate=cost(3),
    )(group.reshape(1), samples)
    columns = lax.all_to_all(columns, TIME, 0, 0, tiled=True)

    block_index = jnp.arange(pattern.shape[1], dtype=jnp.int32)
    active = pattern.astype(F32) * (block_index[None, :] < cutoff[:, None]).astype(F32)
    weight = jnp.repeat(active, SIDE // pattern.shape[1], axis=1)
    masked = jnp.swapaxes(templates.reshape(2, 4, 16, SIDE), 0, 1) * weight
    pieces = spread_templates(masked, y)
    pieces, group, me, place = lax.optimization_barrier((pieces, group, me, place))
    moved = [move_templates(pieces, y, side, step) for step in (0, 1, 2, 3)]

    row = jnp.arange(256, dtype=jnp.int32)[:, None]
    lane = jnp.arange(128, dtype=jnp.int32)[None, :]
    first_phase = phases((256 * group + 8 * me + row % 8) * (row // 8 + 32 * (lane % 64)), -1.0)
    fixed = [jnp.asarray(t) for t in (row_twiddle(), first_table(2), first_table(1))]
    columns, first_phase, fixed = lax.optimization_barrier((columns, first_phase, fixed))

    def first_bins(columns, first_phase, *fixed):
        rows = call(
            first_section,
            shape(RANKS * 24, 128),
            [vmem] * 5,
            [pltpu.VMEM((256, 256), F32), pltpu.VMEM((256, 128), F32), pltpu.VMEM((3, 256, 128), F32)],
            cost_estimate=cost(4),
        )(columns, *fixed, first_phase)
        return lax.all_to_all(rows.reshape(RANKS, 24, 128), BINS, 0, 0, tiled=True)

    rows = lax.cond(place >= 0, first_bins, lambda columns, *rest: columns, columns, first_phase, *fixed)
    rows, moved, place = lax.optimization_barrier((rows, moved, place))
    near = phases(jnp.arange(128, dtype=jnp.int32)[:, None] * (512 * (lane // 16 % 4) + 16 * place + lane % 16), 1.0)
    mix = mixing_tables(place)
    bank, norm = call(
        prepare_templates,
        (shape(2, SIDE, 128), shape(8, 128)),
        [smem] + [anywhere] * 4,
        [pltpu.VMEM((4, 2, 16, SIDE), F32), pltpu.SemaphoreType.DMA((4,))],
        cost_estimate=cost(4),
    )(side.reshape(1), *moved)

    tables = [jnp.asarray(t) for t in (column_table(), digit_twiddle(), fold_twiddle())]
    others, early = lax.optimization_barrier((rows[:, 0:16, :], rows[:, 16:24, :]))
    others = lax.all_gather(others, ("zp", "core"), axis=0)
    pieces, (bank, near, mix) = gather_pieces(early, (bank, near, mix))
    work = [pltpu.VMEM((4, 256, 256), F32), pltpu.VMEM((8, 128, 256), F32)]
    mixing = pltpu.VMEM((2, 8, 256, 256), BF16)
    first = call(
        filter_first,
        shape(RANKS, 72, 128),
        [smem] + [anywhere] * 9 + [vmem] * 6,
        work + [mixing, pltpu.VMEM((GROUPS, RANKS, 8, 128), F32), pltpu.SemaphoreType.DMA((9,))],
        cost_estimate=cost(8),
    )(jnp.stack((side, core)), *pieces, mix, bank, near, *tables, norm)
    first = lax.all_to_all(first, BINS, 0, 0, tiled=True)
    second = call(
        filter_rest,
        shape(RANKS, 128, 128),
        [anywhere] * 7,
        work
        + [
            pltpu.VMEM((2, SIDE, 128), F32),
            pltpu.VMEM((2, 128, 128), F32),
            mixing,
            pltpu.VMEM((2, 2, 256, 256), BF16),
            pltpu.VMEM((8, 2, 128, 128), F32),
            pltpu.VMEM((8, 2, 128), F32),
            pltpu.VMEM((2, GROUPS, RANKS, 8, 128), F32),
            pltpu.SemaphoreType.DMA((8,)),
        ],
        limit=58 * 1024 * 1024,
        cost_estimate=cost(12),
    )(others, bank, near, mix, *tables)
    second = lax.all_to_all(second, BINS, 0, 0, tiled=True)

    twiddle, wide = jnp.asarray(inner_twiddle()), jnp.asarray(last_table())
    work = pltpu.VMEM((1024, 256), F32)
    total = call(start_power, shape(1096, 128), [vmem] * 3, [work], cost_estimate=cost(3))(first, twiddle, wide)
    power = call(finish_power, shape(1024, 128), [vmem] * 3, [work] * 2, cost_estimate=cost(6))(second, wide, total)
    power = power.reshape(4, 256, 128)
    power = [forward(lax.dynamic_index_in_dim(power, (side + step) % 4, 0, False), "zp", step) for step in range(4)]
    best = call(best_template, shape(256, 128), [vmem] * 4, cost_estimate=cost(1))(*power)
    other = lax.ppermute(best, "core", ACROSS)
    power = call(merge_templates, shape(RANKS, 64, 128), [smem] + [vmem] * 6, cost_estimate=cost(2))(
        side.reshape(1), *power, best, other
    )
    power = lax.all_to_all(power, BINS, 0, 0, tiled=True)
    snr, peak = call(place_samples, (shape(1024, 128), shape(1024, 128)), [vmem], cost_estimate=cost(2))(power)
    return snr.reshape(1, 64 * SIDE), peak.reshape(64 * SIDE)


def solution(mesh):
    mesh = jax.sharding.Mesh(mesh.devices.reshape(4, 2, 4, 4, 2), ("zp", "zl", "x", "y", "core"))
    group = ("y", "core")
    in_specs = (P(None, None, TIME), P(None, group, TIME, None), P(group, None), P(group))
    out_specs = (P(group, TIME), P(TIME))
    return jax.shard_map(local, mesh=mesh, in_specs=in_specs, out_specs=out_specs, check_vma=False)
```

```python
import functools
import math

import jax
import jax.numpy as jnp
import numpy as np
from jax import lax
from jax.experimental import pallas as pl
from jax.experimental.pallas import tpu as pltpu
from jax.sharding import PartitionSpec as P

EPSILON = 1e-06
SIDE = 2048
FULL = SIDE * SIDE
DETECTORS = 3
RANKS = 32
GROUPS = 8
F32 = jnp.float32
BF16 = jnp.bfloat16
VMEM_LIMIT = 24 * 1024 * 1024


def split_table(table):
    high = table.astype(np.float32).astype(jnp.bfloat16)
    low = (table - high.astype(np.float64)).astype(np.float32).astype(jnp.bfloat16)
    return np.stack((high, low))


def first_table(copies):
    theta = 2.0 * np.pi * np.outer(np.arange(64), np.arange(64)) / 64.0
    eye = np.eye(copies)
    cosine, sine = np.kron(eye, np.cos(theta)), np.kron(eye, np.sin(theta))
    return split_table(np.block([[cosine, -sine], [sine, cosine]]))


def last_table():
    theta = 2.0 * np.pi * np.outer(np.arange(16), np.arange(16)) / 16.0
    eye = np.eye(8)
    cosine, sine = np.kron(eye, np.cos(theta)), np.kron(eye, np.sin(theta))
    return split_table(np.block([[cosine, sine], [-sine, cosine]]))


def column_table():
    theta = 2.0 * np.pi * np.outer(np.arange(128), np.arange(128)) / 128.0
    cosine, sine = np.cos(theta), np.sin(theta)
    whole = np.block([[cosine, sine], [-sine, cosine]])
    return np.stack((split_table(whole), split_table(whole.T)))


def digit_twiddle():
    digit = 2 * np.arange(8)[:, None, None] + (np.arange(128) // 64)[None, None, :]
    theta = 2.0 * np.pi * (np.arange(128)[None, :, None] * digit) / SIDE
    return np.stack((np.cos(theta), np.sin(theta)), axis=1).astype(np.float32)


def fold_twiddle():
    theta = 2.0 * np.pi * np.outer(np.arange(8), np.arange(128) // 64) / 16.0
    return np.stack((np.cos(theta), -np.sin(theta)), axis=1).astype(np.float32)


def row_twiddle():
    theta = 2.0 * np.pi * np.outer(np.arange(32), np.arange(128) % 64) / SIDE
    return np.stack((np.cos(theta), np.sin(theta))).astype(np.float32)


def inner_twiddle():
    theta = 2.0 * np.pi * np.outer(np.arange(32), np.arange(128) % 16) / 512.0
    return np.stack((np.cos(theta), np.sin(theta))).astype(np.float32)


def phases(turns, orient):
    angle = (turns % FULL).astype(F32) * (orient * 2.0 * math.pi / FULL)
    return jnp.stack((jnp.cos(angle), jnp.sin(angle)))


def mixing_tables(place):
    k = jnp.arange(8, dtype=jnp.int32)[:, None, None]
    into = jnp.arange(128, dtype=jnp.int32)[None, :, None]
    out = jnp.arange(128, dtype=jnp.int32)[None, None, :]
    block, w = k + 8 * (out // 64), out // 16 % 4
    e, a, i = into // 64, into // 16 % 4, into % 16
    turns = e * block * (FULL // 16) + 128 * block * (512 * a + 16 * place + i)
    turns = turns % FULL + a * w * (FULL // 4) + (16 * place + i) * w * SIDE
    cosine, sine = phases(turns, 1.0) * (i == out % 16).astype(F32)
    whole = jnp.concatenate(
        (jnp.concatenate((cosine, sine), axis=2), jnp.concatenate((-sine, cosine), axis=2)), axis=1
    )
    high = lax.reduce_precision(whole, 8, 7)
    return jnp.stack((high.astype(BF16), (whole - high).astype(BF16)))


def times_unit(value, numer, denom, orient):
    re, im = value
    numer = numer % denom
    if numer == 0:
        return value
    if 8 * numer % denom == 0:
        eighth = 8 * numer // denom
        if eighth == 4:
            return -re, -im
        if eighth in (2, 6):
            return (-im, re) if (eighth == 2) == (orient > 0) else (im, -re)
    cosine = math.cos(2.0 * math.pi * numer / denom)
    sine = orient * math.sin(2.0 * math.pi * numer / denom)
    return re * cosine - im * sine, re * sine + im * cosine


def butterfly(values, orient):
    count = len(values)
    if count == 1:
        return values
    if count == 2:
        (ar, ai), (br, bi) = values
        return [(ar + br, ai + bi), (ar - br, ai - bi)]
    if count == 4:
        (ar, ai), (br, bi), (cr, ci), (dr, di) = values
        sr, si, tr, ti = ar + cr, ai + ci, ar - cr, ai - ci
        ur, ui, vr, vi = br + dr, bi + di, br - dr, bi - di
        if orient > 0:
            return [(sr + ur, si + ui), (tr - vi, ti + vr), (sr - ur, si - ui), (tr + vi, ti - vr)]
        return [(sr + ur, si + ui), (tr + vi, ti - vr), (sr - ur, si - ui), (tr - vi, ti + vr)]
    radix = 4 if count % 4 == 0 else 2
    inner = count // radix
    parts = [butterfly(values[s::radix], orient) for s in range(radix)]
    out = [None] * count
    for k in range(inner):
        joined = butterfly([times_unit(parts[s][k], s * k, count, orient) for s in range(radix)], orient)
        for part in range(radix):
            out[k + inner * part] = joined[part]
    return out


def halves(value):
    high = value.astype(BF16)
    return high, (value - high.astype(F32)).astype(BF16)


def dot(a, b, contract=((1,), (0,))):
    return lax.dot_general(a, b, (contract, ((), ())), preferred_element_type=F32)


def low_lanes(shape):
    return lax.broadcasted_iota(jnp.int32, shape, 1) < 64


def swap(value):
    return pltpu.roll(value, 64, 1)


def fetch(pairs, sems):
    copies = [pltpu.make_async_copy(source, target, sems.at[at]) for at, (source, target) in enumerate(pairs)]
    for copy in copies:
        copy.start()
    return copies


def tile_rows(start):
    return pl.ds(pl.multiple_of(start, 8), 8)


def gather_columns(group_ref, strain_ref, out_ref):
    first = 4 * lax.rem(group_ref[0], 2)

    def piece(detector, tile, part):
        return strain_ref[pl.ds(512 * detector + first + 2 * tile + part, 64, stride=8), :]

    for tile in range(2):
        for at, (one, two) in enumerate((((0, 0), (1, 0)), ((0, 1), (1, 1)), ((2, 0), (2, 1)))):
            joined = jnp.concatenate((piece(one[0], tile, one[1]), piece(two[0], tile, two[1])), axis=0)
            out_ref[16 * tile:16 * tile + 16, 8 * at:8 * at + 8, :] = joined.T.reshape(16, 8, 128)


def prepare_templates(side_ref, *refs):
    pieces, (out_ref, norm_ref, held_ref, sems) = refs[:4], refs[4:]
    copies = []
    for at, piece in enumerate(pieces):
        copy = pltpu.make_async_copy(piece, held_ref.at[lax.rem(side_ref[0] + (4 - at), 4)], sems.at[at])
        copy.start()
        copies.append(copy)
    for copy in copies:
        copy.wait()
    total = jnp.zeros((64, 128), F32)
    for chunk in range(16):
        lanes = slice(128 * chunk, 128 * chunk + 128)
        for part in range(2):
            value = jnp.concatenate([held_ref[a, part, :, lanes] for a in range(4)], axis=0)
            total = total + value * value
            out_ref[part, lanes, :] = jnp.concatenate((value, pltpu.roll(value, 127, 1)), axis=0).T
    norm_ref[...] = jnp.sum(total.reshape(8, 8, 128), axis=0)


def first_section(in_ref, twiddle_ref, wide_ref, narrow_ref, phase_ref, out_ref, pair_ref, single_ref, turn_ref):
    lower = low_lanes((8, 128))
    for at in range(2):
        values = []
        for rank in range(RANKS):
            if at == 0:
                values.append((in_ref[rank, 0:8, :], in_ref[rank, 8:16, :]))
            else:
                one = in_ref[rank, 16:24, :]
                values.append((one, swap(one)))
        for digit, (re, im) in enumerate(butterfly(values, -1)):
            cosine, sine = twiddle_ref[0, digit:digit + 1, :], twiddle_ref[1, digit:digit + 1, :]
            re, im = re * cosine + im * sine, im * cosine - re * sine
            rows = slice(8 * digit, 8 * digit + 8)
            if at == 0:
                pair_ref[rows, 0:128] = re
                pair_ref[rows, 128:256] = im
            else:
                single_ref[rows, :] = jnp.where(lower, re, swap(im))
    high, low = halves(pair_ref[...])
    pair = dot(high, wide_ref[0]) + dot(low, wide_ref[0]) + dot(high, wide_ref[1])
    high, low = halves(single_ref[...])
    single = dot(high, narrow_ref[0]) + dot(low, narrow_ref[0]) + dot(high, narrow_ref[1])
    cosine, sine = phase_ref[0], phase_ref[1]
    re, im = pair[:, 0:128], pair[:, 128:256]
    turn_ref[0] = re * cosine - im * sine
    turn_ref[1] = im * cosine + re * sine
    turn_ref[2] = single * cosine + swap(single) * jnp.where(low_lanes((256, 128)), -sine, sine)
    for at in range(DETECTORS):
        for quad in range(2):
            blocks = []
            for part in range(2):
                source, start = (part, 64 * at) if at < 2 else (2, 64 * part)
                cols = [turn_ref[source, pl.ds(4 * quad + u, 32, stride=8), :] for u in range(4)]
                for a in range(4):
                    lanes = slice(start + 16 * a, start + 16 * a + 16)
                    blocks.append(jnp.concatenate([c[16 * h:16 * h + 16, lanes] for c in cols for h in range(2)], axis=1))
            turned = jnp.concatenate(blocks, axis=0).T
            for u in range(4):
                for h in range(2):
                    rows = pl.ds(24 * h + 8 * at + 4 * quad + u, 16, stride=48)
                    out_ref[rows, :] = turned[32 * u + 16 * h:32 * u + 16 * h + 16, :]


def slot_of(a, low):
    return 4 * (a % 2) + 2 * (low // 8) + a // 2 % 2, 16 * (low // 4 % 2) + 4 * (low % 4) + a // 4


def filter_detector(
    load, template_ref, near_ref, mix_ref, table_ref, digit_ref, fold_ref, out_ref, base, work_ref, last_ref, waits
):
    lower = low_lanes((8, 128))

    def spread(low, carry):
        values = []
        for a in range(8):
            one = load(*slot_of(a, low))
            two = load(*slot_of(a + 8, low))
            add, sub = one + two, one - two
            re, im = jnp.where(lower, add, swap(sub)), jnp.where(lower, swap(add), sub)
            cosine, sine = fold_ref[a, 0:1, :], fold_ref[a, 1:2, :]
            values.append((re * cosine - im * sine, re * sine + im * cosine) if a else (re, im))
        for pair, (re, im) in enumerate(butterfly(values, -1)):
            cosine, sine = digit_ref[pair, 0, tile_rows(8 * low), :], digit_ref[pair, 1, tile_rows(8 * low), :]
            lanes = slice(128 * (pair % 2), 128 * (pair % 2) + 128)
            work_ref[pair // 2, tile_rows(8 * low), lanes] = re * cosine + im * sine
            work_ref[pair // 2, tile_rows(128 + 8 * low), lanes] = im * cosine - re * sine
        return carry

    lax.fori_loop(0, 16, spread, 0, unroll=2)
    for copy in waits[0]:
        copy.wait()

    for quad in range(4):
        high, low = halves(work_ref[quad])
        spectrum = dot(table_ref[0, 0], high) + dot(table_ref[0, 0], low) + dot(table_ref[0, 1], high)
        s_re, s_im = spectrum[0:128], spectrum[128:256]
        rows = [pl.ds(4 * quad + 2 * k, 128, stride=16) for k in range(2)]
        h_re = jnp.concatenate([template_ref[0, r, :] for r in rows], axis=1)
        h_im = jnp.concatenate([template_ref[1, r, :] for r in rows], axis=1)
        product = jnp.concatenate((s_re * h_re + s_im * h_im, s_im * h_re - s_re * h_im), axis=0)
        high, low = halves(product)
        series = dot(table_ref[1, 0], high) + dot(table_ref[1, 0], low) + dot(table_ref[1, 1], high)
        for k in range(2):
            lanes = slice(128 * k, 128 * k + 128)
            re, im = series[0:128, lanes], series[128:256, lanes]
            cosine, sine = digit_ref[2 * quad + k, 0], digit_ref[2 * quad + k, 1]
            re, im = re * cosine - im * sine, re * sine + im * cosine
            cosine, sine = near_ref[0], near_ref[1]
            work_ref[quad, 0:128, lanes] = re * cosine - im * sine
            work_ref[quad, 128:256, lanes] = re * sine + im * cosine

    def collect(step, carry):
        values = []
        for pair in range(8):
            lanes = slice(128 * (pair % 2), 128 * (pair % 2) + 128)
            rows = tile_rows(8 * step), tile_rows(128 + 8 * step)
            values.append((work_ref[pair // 2, rows[0], lanes], work_ref[pair // 2, rows[1], lanes]))
        for k, (re, im) in enumerate(butterfly(values, 1)):
            last_ref[k, tile_rows(8 * step), 0:128] = re
            last_ref[k, tile_rows(8 * step), 128:256] = im
        return carry

    lax.fori_loop(0, 16, collect, 0, unroll=2)
    for copy in waits[1]:
        copy.wait()
    for k in range(8):
        high, low = halves(last_ref[k])
        mixed = dot(high, mix_ref[0, k]) + dot(low, mix_ref[0, k]) + dot(high, mix_ref[1, k])
        for quarter in range(4):
            rows = slice(32 * quarter, 32 * quarter + 32)
            out_ref[4 * k + quarter, base:base + 32, :] = mixed[rows, 0:128]
            out_ref[4 * k + quarter, base + 32:base + 64, :] = mixed[rows, 128:256]


def filter_first(member_ref, *refs):
    pieces, mix_hbm, tables, norm_ref = refs[:10], refs[10], refs[11:16], refs[16]
    out_ref, work_ref, last_ref, mix_ref, held_ref, sems = refs[17:]
    side, core = member_ref[0], member_ref[1]
    pairs = []
    for at, piece in enumerate(pieces):
        step, first = ((0, 0), (3, 0), (1, 0), (2, 0), (2, 16))[at % 5]
        slot = 2 * lax.rem(side + step, 4) + (core if at < 5 else 1 - core)
        pairs.append((piece, held_ref.at[slot, pl.ds(first, piece.shape[0])]))
    copies = fetch(pairs + [(mix_hbm, mix_ref)], sems)
    for rank in range(RANKS):
        out_ref[rank, 64:72, :] = norm_ref[...]
    for copy in copies[:10]:
        copy.wait()
    bank_ref, near_ref, table_ref, digit_ref, fold_ref = tables
    filter_detector(
        lambda member, rank: held_ref[member, rank],
        bank_ref, near_ref, mix_ref, table_ref, digit_ref, fold_ref, out_ref, 0, work_ref, last_ref, ((), copies[10:]),
    )


def filter_rest(in_hbm, bank_hbm, near_hbm, mix_hbm, table_hbm, digit_hbm, fold_hbm, out_ref, *scratch):
    work_ref, last_ref, bank_ref, near_ref, mix_ref, table_ref, digit_ref, fold_ref, held_ref, sems = scratch
    pairs = [(in_hbm.at[:, :, 8 * at:8 * at + 8, :], held_ref.at[at]) for at in range(2)]
    pairs = [pairs[0], (fold_hbm, fold_ref), (digit_hbm, digit_ref), (table_hbm, table_ref), (bank_hbm, bank_ref)] + [
        (near_hbm, near_ref), (mix_hbm, mix_ref), pairs[1]
    ]
    copies = fetch(pairs, sems)
    for copy in copies[:3]:
        copy.wait()
    for at in range(2):
        filter_detector(
            lambda member, rank, at=at: held_ref[at, member, rank],
            bank_ref, near_ref, mix_ref, table_ref, digit_ref, fold_ref, out_ref, 64 * at, work_ref, last_ref,
            ((), ()) if at else (copies[3:6], copies[6:8]),
        )


def detector_power(in_ref, base, twiddle_ref, wide_ref, work_ref):
    def step_fn(step, carry):
        values = [
            (in_ref[r, tile_rows(base + 8 * step), :], in_ref[r, tile_rows(base + 32 + 8 * step), :])
            for r in range(RANKS)
        ]
        for digit, (re, im) in enumerate(butterfly(values, 1)):
            cosine, sine = twiddle_ref[0, digit:digit + 1, :], twiddle_ref[1, digit:digit + 1, :]
            at = 16 * (digit // 16) + 4 * (digit % 4) + digit // 4 % 4
            rows = tile_rows(32 * at + 8 * step)
            work_ref[rows, 0:128] = re * cosine - im * sine
            work_ref[rows, 128:256] = im * cosine + re * sine
        return carry

    lax.fori_loop(0, 4, step_fn, 0)

    def power_of(quad):
        high, low = halves(work_ref[pl.ds(pl.multiple_of(128 * quad, 128), 128), :])
        full = dot(high, wide_ref[0]) + dot(low, wide_ref[0]) + dot(high, wide_ref[1])
        re, im = full[:, 0:128], full[:, 128:256]
        return re * re + im * im

    return power_of


def start_power(in_ref, twiddle_ref, wide_ref, out_ref, work_ref):
    total = jnp.zeros((8, 128), F32)
    for rank in range(RANKS):
        total = total + in_ref[rank, 64:72, :]
    out_ref[1024:1032, :] = total
    out_ref[1032:1096, :] = twiddle_ref[...].reshape(64, 128)
    power_of = detector_power(in_ref, 0, twiddle_ref, wide_ref, work_ref)

    def step_fn(quad, carry):
        out_ref[pl.ds(pl.multiple_of(128 * quad, 128), 128), :] = power_of(quad)
        return carry

    lax.fori_loop(0, 8, step_fn, 0)


def finish_power(in_ref, wide_ref, sum_ref, out_ref, one_ref, two_ref):
    twiddle_ref = sum_ref.at[1032:1096].reshape(2, 32, 128)
    first = detector_power(in_ref, 0, twiddle_ref, wide_ref, one_ref)
    second = detector_power(in_ref, 64, twiddle_ref, wide_ref, two_ref)
    scale = 1.0 / (FULL * (jnp.sum(sum_ref[1024:1032, :]) + EPSILON))
    for quad in range(8):
        rows = slice(128 * quad, 128 * quad + 128)
        turned = ((first(quad) + second(quad) + sum_ref[rows, :]) * scale).T
        for g in range(8):
            start = 32 * (quad // 4) + 4 * (quad % 4) + 16 * (g // 4) + g % 4
            out_ref[pl.ds(start, 16, stride=64), :] = turned[16 * g:16 * g + 16, :]


def best_template(*refs):
    refs[4][...] = jnp.maximum(jnp.maximum(refs[0][...], refs[1][...]), jnp.maximum(refs[2][...], refs[3][...]))


def merge_templates(side_ref, *refs):
    one_ref, two_ref, out_ref = refs[4:]
    for block in range(8):
        rows = slice(32 * block, 32 * block + 32)
        best = jnp.maximum(one_ref[rows, :], two_ref[rows, :])
        for step in range(4):
            t = lax.rem(side_ref[0] + (4 - step), 4)
            out_ref[4 * block + t, 0:32, :] = refs[step][rows, :]
            out_ref[4 * block + t, 32:64, :] = best


def place_samples(in_ref, out_ref, best_ref):
    for k in range(8):
        for first, target in ((0, out_ref), (32, best_ref)):
            parts = [in_ref[4 * k + quarter, first:first + 32, :] for quarter in range(4)]
            for u in range(4):
                joined = jnp.concatenate([p[:, 32 * u:32 * u + 32] for p in parts], axis=1)
                for h in range(2):
                    target[pl.ds(256 * u + 8 * h + k, 16, stride=16), :] = joined[16 * h:16 * h + 16]


def shape(*dims):
    return jax.ShapeDtypeStruct(dims, F32)


def call(kernel, out, specs, scratch=(), limit=VMEM_LIMIT, **kwargs):
    many = isinstance(out, (tuple, list))
    whole = pl.BlockSpec(memory_space=pltpu.VMEM)
    return pl.pallas_call(
        kernel,
        out_shape=out,
        in_specs=specs,
        out_specs=[whole] * len(out) if many else whole,
        scratch_shapes=list(scratch),
        compiler_params=pltpu.CompilerParams(vmem_limit_bytes=limit),
        **kwargs,
    )


def cost(us):
    return pl.CostEstimate(flops=int(us * 1e9), bytes_accessed=int(us * 1e6), transcendentals=0)


TIME = ("zp", "zl", "x")
BINS = ("zl", "x", "y")
ACROSS = [(0, 1), (1, 0)]


def forward(value, axis, step):
    return lax.ppermute(value, axis, [(i, (i + step) % 4) for i in range(4)]) if step else value


def gather_pieces(value, ready):
    half = value.shape[0] // 2
    back, ahead = forward(value, "zp", 1), forward(value, "zp", 3)
    own = [value, back, ahead, forward(back[:half], "zp", 1), forward(ahead[half:], "zp", 3)]
    own, ready = lax.optimization_barrier((own, ready))
    return own + [lax.ppermute(one, "core", ACROSS) for one in own], ready


def spread_templates(masked, y):
    pieces = [lax.dynamic_index_in_dim(masked, y, 0, False)]
    for step in (1, 2, 3):
        pieces.append(forward(lax.dynamic_index_in_dim(masked, (y + step) % 4, 0, False), "y", step))
    return jnp.stack(pieces)


def move_templates(pieces, y, side, step):
    return forward(lax.dynamic_index_in_dim(pieces, (y - side - step) % 4, 0, False), "zp", step)


def local(strain, templates, pattern, cutoff):
    side, low, x, y, core = (lax.axis_index(n).astype(jnp.int32) for n in ("zp", "zl", "x", "y", "core"))
    me, group, place = 8 * side + 4 * low + x, 2 * y + core, 16 * low + 4 * x + y
    vmem = pl.BlockSpec(memory_space=pltpu.VMEM)
    smem = pl.BlockSpec(memory_space=pltpu.SMEM)
    anywhere = pl.BlockSpec(memory_space=pl.ANY)

    samples = strain.reshape(2, 3, 64, 16, 128).transpose(1, 2, 3, 0, 4).reshape(192, 32, 128)
    columns = pl.pallas_call(
        lambda group_ref, strain_ref, out_ref: gather_columns(group_ref, strain_ref.reshape(1536, 128), out_ref),
        out_shape=shape(RANKS, 24, 128),
        grid_spec=pltpu.PrefetchScalarGridSpec(
            num_scalar_prefetch=1,
            grid=(1,),
            in_specs=[pl.BlockSpec((192, 8, 128), lambda i, at: (0, at[0] // 2, 0))],
            out_specs=pl.BlockSpec((RANKS, 24, 128), lambda i, at: (0, 0, 0)),
        ),
        compiler_params=pltpu.CompilerParams(vmem_limit_bytes=58 * 1024 * 1024),
        cost_estimate=cost(3),
    )(group.reshape(1), samples)
    columns, templates = lax.optimization_barrier((columns, templates))
    columns = lax.all_to_all(columns, TIME, 0, 0, tiled=True)

    block_index = jnp.arange(pattern.shape[1], dtype=jnp.int32)
    active = pattern.astype(F32) * (block_index[None, :] < cutoff[:, None]).astype(F32)
    weight = jnp.repeat(active, SIDE // pattern.shape[1], axis=1)
    masked = jnp.swapaxes(templates.reshape(2, 4, 16, SIDE), 0, 1) * weight
    pieces = spread_templates(masked, y)
    pieces, group, me, place = lax.optimization_barrier((pieces, group, me, place))
    moved = [move_templates(pieces, y, side, step) for step in (0, 1, 2, 3)]

    row = jnp.arange(256, dtype=jnp.int32)[:, None]
    lane = jnp.arange(128, dtype=jnp.int32)[None, :]
    first_phase = phases((256 * group + 8 * me + row % 8) * (row // 8 + 32 * (lane % 64)), -1.0)
    fixed = [jnp.asarray(t) for t in (row_twiddle(), first_table(2), first_table(1))]
    columns, first_phase, fixed = lax.optimization_barrier((columns, first_phase, fixed))

    def first_bins(columns, first_phase, *fixed):
        rows = call(
            first_section,
            shape(RANKS * 24, 128),
            [vmem] * 5,
            [pltpu.VMEM((256, 256), F32), pltpu.VMEM((256, 128), F32), pltpu.VMEM((3, 256, 128), F32)],
            cost_estimate=cost(4),
        )(columns, *fixed, first_phase)
        return lax.all_to_all(rows.reshape(RANKS, 24, 128), BINS, 0, 0, tiled=True)

    rows = lax.cond(place >= 0, first_bins, lambda columns, *rest: columns, columns, first_phase, *fixed)
    rows, moved, place = lax.optimization_barrier((rows, moved, place))
    near = phases(jnp.arange(128, dtype=jnp.int32)[:, None] * (512 * (lane // 16 % 4) + 16 * place + lane % 16), 1.0)
    mix = mixing_tables(place)
    bank, norm = call(
        prepare_templates,
        (shape(2, SIDE, 128), shape(8, 128)),
        [smem] + [anywhere] * 4,
        [pltpu.VMEM((4, 2, 16, SIDE), F32), pltpu.SemaphoreType.DMA((4,))],
        cost_estimate=cost(4),
    )(side.reshape(1), *moved)

    tables = [jnp.asarray(t) for t in (column_table(), digit_twiddle(), fold_twiddle())]
    others, early = lax.optimization_barrier((rows[:, 0:16, :], rows[:, 16:24, :]))
    others = lax.all_gather(others, ("zp", "core"), axis=0)
    pieces, (bank, near, mix) = gather_pieces(early, (bank, near, mix))
    work = [pltpu.VMEM((4, 256, 256), F32), pltpu.VMEM((8, 128, 256), F32)]
    mixing = pltpu.VMEM((2, 8, 256, 256), BF16)
    first = call(
        filter_first,
        shape(RANKS, 72, 128),
        [smem] + [anywhere] * 11 + [vmem] * 6,
        work + [mixing, pltpu.VMEM((GROUPS, RANKS, 8, 128), F32), pltpu.SemaphoreType.DMA((11,))],
        cost_estimate=cost(8),
    )(jnp.stack((side, core)), *pieces, mix, bank, near, *tables, norm)
    first = lax.all_to_all(first, BINS, 0, 0, tiled=True)
    second = call(
        filter_rest,
        shape(RANKS, 128, 128),
        [anywhere] * 7,
        work
        + [
            pltpu.VMEM((2, SIDE, 128), F32),
            pltpu.VMEM((2, 128, 128), F32),
            mixing,
            pltpu.VMEM((2, 2, 256, 256), BF16),
            pltpu.VMEM((8, 2, 128, 128), F32),
            pltpu.VMEM((8, 2, 128), F32),
            pltpu.VMEM((2, GROUPS, RANKS, 8, 128), F32),
            pltpu.SemaphoreType.DMA((8,)),
        ],
        limit=58 * 1024 * 1024,
        cost_estimate=cost(12),
    )(others, bank, near, mix, *tables)
    second = lax.all_to_all(second, BINS, 0, 0, tiled=True)

    twiddle, wide = jnp.asarray(inner_twiddle()), jnp.asarray(last_table())
    work = pltpu.VMEM((1024, 256), F32)
    total = call(start_power, shape(1096, 128), [vmem] * 3, [work], cost_estimate=cost(3))(first, twiddle, wide)
    power = call(finish_power, shape(1024, 128), [vmem] * 3, [work] * 2, cost_estimate=cost(6))(second, wide, total)
    power = power.reshape(4, 256, 128)
    power = [forward(lax.dynamic_index_in_dim(power, (side + step) % 4, 0, False), "zp", step) for step in range(4)]
    best = call(best_template, shape(256, 128), [vmem] * 4, cost_estimate=cost(1))(*power)
    other = lax.ppermute(best, "core", ACROSS)
    power = call(merge_templates, shape(RANKS, 64, 128), [smem] + [vmem] * 6, cost_estimate=cost(2))(
        side.reshape(1), *power, best, other
    )
    power = lax.all_to_all(power, BINS, 0, 0, tiled=True)
    snr, peak = call(place_samples, (shape(1024, 128), shape(1024, 128)), [vmem], cost_estimate=cost(2))(power)
    return snr.reshape(1, 64 * SIDE), peak.reshape(64 * SIDE)


def solution(mesh):
    mesh = jax.sharding.Mesh(mesh.devices.reshape(4, 2, 4, 4, 2), ("zp", "zl", "x", "y", "core"))
    group = ("y", "core")
    in_specs = (P(None, None, TIME), P(None, group, TIME, None), P(group, None), P(group))
    out_specs = (P(group, TIME), P(TIME))
    return jax.shard_map(local, mesh=mesh, in_specs=in_specs, out_specs=out_specs, check_vma=False)
```

```python
import functools
import math

import jax
import jax.numpy as jnp
import numpy as np
from jax import lax
from jax.experimental import pallas as pl
from jax.experimental.pallas import tpu as pltpu
from jax.sharding import PartitionSpec as P

EPSILON = 1e-06
SIDE = 2048
FULL = SIDE * SIDE
DETECTORS = 3
RANKS = 32
GROUPS = 8
F32 = jnp.float32
BF16 = jnp.bfloat16
VMEM_LIMIT = 24 * 1024 * 1024


def split_table(table):
    high = table.astype(np.float32).astype(jnp.bfloat16)
    low = (table - high.astype(np.float64)).astype(np.float32).astype(jnp.bfloat16)
    return np.stack((high, low))


def first_table(copies):
    theta = 2.0 * np.pi * np.outer(np.arange(64), np.arange(64)) / 64.0
    eye = np.eye(copies)
    cosine, sine = np.kron(eye, np.cos(theta)), np.kron(eye, np.sin(theta))
    return split_table(np.block([[cosine, -sine], [sine, cosine]]))


def last_table():
    theta = 2.0 * np.pi * np.outer(np.arange(16), np.arange(16)) / 16.0
    eye = np.eye(8)
    cosine, sine = np.kron(eye, np.cos(theta)), np.kron(eye, np.sin(theta))
    return split_table(np.block([[cosine, sine], [-sine, cosine]]))


def column_table():
    theta = 2.0 * np.pi * np.outer(np.arange(128), np.arange(128)) / 128.0
    cosine, sine = np.cos(theta), np.sin(theta)
    whole = np.block([[cosine, sine], [-sine, cosine]])
    return np.stack((split_table(whole), split_table(whole.T)))


def digit_twiddle():
    digit = 2 * np.arange(8)[:, None, None] + (np.arange(128) // 64)[None, None, :]
    theta = 2.0 * np.pi * (np.arange(128)[None, :, None] * digit) / SIDE
    return np.stack((np.cos(theta), np.sin(theta)), axis=1).astype(np.float32)


def fold_twiddle():
    theta = 2.0 * np.pi * np.outer(np.arange(8), np.arange(128) // 64) / 16.0
    return np.stack((np.cos(theta), -np.sin(theta)), axis=1).astype(np.float32)


def row_twiddle():
    theta = 2.0 * np.pi * np.outer(np.arange(32), np.arange(128) % 64) / SIDE
    return np.stack((np.cos(theta), np.sin(theta))).astype(np.float32)


def inner_twiddle():
    theta = 2.0 * np.pi * np.outer(np.arange(32), np.arange(128) % 16) / 512.0
    return np.stack((np.cos(theta), np.sin(theta))).astype(np.float32)


def phases(turns, orient):
    angle = (turns % FULL).astype(F32) * (orient * 2.0 * math.pi / FULL)
    return jnp.stack((jnp.cos(angle), jnp.sin(angle)))


def mixing_tables(place):
    k = jnp.arange(8, dtype=jnp.int32)[:, None, None]
    into = jnp.arange(128, dtype=jnp.int32)[None, :, None]
    out = jnp.arange(128, dtype=jnp.int32)[None, None, :]
    block, w = k + 8 * (out // 64), out // 16 % 4
    e, a, i = into // 64, into // 16 % 4, into % 16
    turns = e * block * (FULL // 16) + 128 * block * (512 * a + 16 * place + i)
    turns = turns % FULL + a * w * (FULL // 4) + (16 * place + i) * w * SIDE
    cosine, sine = phases(turns, 1.0) * (i == out % 16).astype(F32)
    whole = jnp.concatenate(
        (jnp.concatenate((cosine, sine), axis=2), jnp.concatenate((-sine, cosine), axis=2)), axis=1
    )
    high = lax.reduce_precision(whole, 8, 7)
    return jnp.stack((high.astype(BF16), (whole - high).astype(BF16)))


def times_unit(value, numer, denom, orient):
    re, im = value
    numer = numer % denom
    if numer == 0:
        return value
    if 8 * numer % denom == 0:
        eighth = 8 * numer // denom
        if eighth == 4:
            return -re, -im
        if eighth in (2, 6):
            return (-im, re) if (eighth == 2) == (orient > 0) else (im, -re)
    cosine = math.cos(2.0 * math.pi * numer / denom)
    sine = orient * math.sin(2.0 * math.pi * numer / denom)
    return re * cosine - im * sine, re * sine + im * cosine


def butterfly(values, orient):
    count = len(values)
    if count == 1:
        return values
    if count == 2:
        (ar, ai), (br, bi) = values
        return [(ar + br, ai + bi), (ar - br, ai - bi)]
    if count == 4:
        (ar, ai), (br, bi), (cr, ci), (dr, di) = values
        sr, si, tr, ti = ar + cr, ai + ci, ar - cr, ai - ci
        ur, ui, vr, vi = br + dr, bi + di, br - dr, bi - di
        if orient > 0:
            return [(sr + ur, si + ui), (tr - vi, ti + vr), (sr - ur, si - ui), (tr + vi, ti - vr)]
        return [(sr + ur, si + ui), (tr + vi, ti - vr), (sr - ur, si - ui), (tr - vi, ti + vr)]
    radix = 4 if count % 4 == 0 else 2
    inner = count // radix
    parts = [butterfly(values[s::radix], orient) for s in range(radix)]
    out = [None] * count
    for k in range(inner):
        joined = butterfly([times_unit(parts[s][k], s * k, count, orient) for s in range(radix)], orient)
        for part in range(radix):
            out[k + inner * part] = joined[part]
    return out


def halves(value):
    high = value.astype(BF16)
    return high, (value - high.astype(F32)).astype(BF16)


def dot(a, b, contract=((1,), (0,))):
    return lax.dot_general(a, b, (contract, ((), ())), preferred_element_type=F32)


def low_lanes(shape):
    return lax.broadcasted_iota(jnp.int32, shape, 1) < 64


def swap(value):
    return pltpu.roll(value, 64, 1)


def fetch(pairs, sems):
    copies = [pltpu.make_async_copy(source, target, sems.at[at]) for at, (source, target) in enumerate(pairs)]
    for copy in copies:
        copy.start()
    return copies


def tile_rows(start):
    return pl.ds(pl.multiple_of(start, 8), 8)


def gather_columns(group_ref, strain_ref, out_ref):
    first = 4 * lax.rem(group_ref[0], 2)

    def piece(detector, tile, part):
        return strain_ref[pl.ds(512 * detector + first + 2 * tile + part, 64, stride=8), :]

    for tile in range(2):
        for at, (one, two) in enumerate((((0, 0), (1, 0)), ((0, 1), (1, 1)), ((2, 0), (2, 1)))):
            joined = jnp.concatenate((piece(one[0], tile, one[1]), piece(two[0], tile, two[1])), axis=0)
            out_ref[16 * tile:16 * tile + 16, 8 * at:8 * at + 8, :] = joined.T.reshape(16, 8, 128)


def prepare_templates(side_ref, *refs):
    pieces, (out_ref, norm_ref, held_ref, sems) = refs[:4], refs[4:]
    copies = []
    for at, piece in enumerate(pieces):
        copy = pltpu.make_async_copy(piece, held_ref.at[lax.rem(side_ref[0] + (4 - at), 4)], sems.at[at])
        copy.start()
        copies.append(copy)
    for copy in copies:
        copy.wait()
    total = jnp.zeros((64, 128), F32)
    for chunk in range(16):
        lanes = slice(128 * chunk, 128 * chunk + 128)
        for part in range(2):
            value = jnp.concatenate([held_ref[a, part, :, lanes] for a in range(4)], axis=0)
            total = total + value * value
            out_ref[part, lanes, :] = jnp.concatenate((value, pltpu.roll(value, 127, 1)), axis=0).T
    norm_ref[...] = jnp.sum(total.reshape(8, 8, 128), axis=0)


def first_section(in_ref, twiddle_ref, wide_ref, narrow_ref, phase_ref, out_ref, pair_ref, single_ref, turn_ref):
    lower = low_lanes((8, 128))
    for at in range(2):
        values = []
        for rank in range(RANKS):
            if at == 0:
                values.append((in_ref[rank, 0:8, :], in_ref[rank, 8:16, :]))
            else:
                one = in_ref[rank, 16:24, :]
                values.append((one, swap(one)))
        for digit, (re, im) in enumerate(butterfly(values, -1)):
            cosine, sine = twiddle_ref[0, digit:digit + 1, :], twiddle_ref[1, digit:digit + 1, :]
            re, im = re * cosine + im * sine, im * cosine - re * sine
            rows = slice(8 * digit, 8 * digit + 8)
            if at == 0:
                pair_ref[rows, 0:128] = re
                pair_ref[rows, 128:256] = im
            else:
                single_ref[rows, :] = jnp.where(lower, re, swap(im))
    high, low = halves(pair_ref[...])
    pair = dot(high, wide_ref[0]) + dot(low, wide_ref[0]) + dot(high, wide_ref[1])
    high, low = halves(single_ref[...])
    single = dot(high, narrow_ref[0]) + dot(low, narrow_ref[0]) + dot(high, narrow_ref[1])
    cosine, sine = phase_ref[0], phase_ref[1]
    re, im = pair[:, 0:128], pair[:, 128:256]
    turn_ref[0] = re * cosine - im * sine
    turn_ref[1] = im * cosine + re * sine
    turn_ref[2] = single * cosine + swap(single) * jnp.where(low_lanes((256, 128)), -sine, sine)
    for at in range(DETECTORS):
        for quad in range(2):
            blocks = []
            for part in range(2):
                source, start = (part, 64 * at) if at < 2 else (2, 64 * part)
                cols = [turn_ref[source, pl.ds(4 * quad + u, 32, stride=8), :] for u in range(4)]
                for a in range(4):
                    lanes = slice(start + 16 * a, start + 16 * a + 16)
                    blocks.append(jnp.concatenate([c[16 * h:16 * h + 16, lanes] for c in cols for h in range(2)], axis=1))
            turned = jnp.concatenate(blocks, axis=0).T
            for u in range(4):
                for h in range(2):
                    rows = pl.ds(24 * h + 8 * at + 4 * quad + u, 16, stride=48)
                    out_ref[rows, :] = turned[32 * u + 16 * h:32 * u + 16 * h + 16, :]


def slot_of(a, low):
    return 4 * (a % 2) + 2 * (low // 8) + a // 2 % 2, 16 * (low // 4 % 2) + 4 * (low % 4) + a // 4


def filter_detector(
    load, template_ref, near_ref, mix_ref, table_ref, digit_ref, fold_ref, out_ref, base, work_ref, last_ref, waits
):
    lower = low_lanes((8, 128))

    def spread(low, carry):
        values = []
        for a in range(8):
            one = load(*slot_of(a, low))
            two = load(*slot_of(a + 8, low))
            add, sub = one + two, one - two
            re, im = jnp.where(lower, add, swap(sub)), jnp.where(lower, swap(add), sub)
            cosine, sine = fold_ref[a, 0:1, :], fold_ref[a, 1:2, :]
            values.append((re * cosine - im * sine, re * sine + im * cosine) if a else (re, im))
        for pair, (re, im) in enumerate(butterfly(values, -1)):
            cosine, sine = digit_ref[pair, 0, tile_rows(8 * low), :], digit_ref[pair, 1, tile_rows(8 * low), :]
            lanes = slice(128 * (pair % 2), 128 * (pair % 2) + 128)
            work_ref[pair // 2, tile_rows(8 * low), lanes] = re * cosine + im * sine
            work_ref[pair // 2, tile_rows(128 + 8 * low), lanes] = im * cosine - re * sine
        return carry

    lax.fori_loop(0, 16, spread, 0, unroll=4)
    for copy in waits[0]:
        copy.wait()

    for quad in range(4):
        high, low = halves(work_ref[quad])
        spectrum = dot(table_ref[0, 0], high) + dot(table_ref[0, 0], low) + dot(table_ref[0, 1], high)
        s_re, s_im = spectrum[0:128], spectrum[128:256]
        rows = [pl.ds(4 * quad + 2 * k, 128, stride=16) for k in range(2)]
        h_re = jnp.concatenate([template_ref[0, r, :] for r in rows], axis=1)
        h_im = jnp.concatenate([template_ref[1, r, :] for r in rows], axis=1)
        product = jnp.concatenate((s_re * h_re + s_im * h_im, s_im * h_re - s_re * h_im), axis=0)
        high, low = halves(product)
        series = dot(table_ref[1, 0], high) + dot(table_ref[1, 0], low) + dot(table_ref[1, 1], high)
        for k in range(2):
            lanes = slice(128 * k, 128 * k + 128)
            re, im = series[0:128, lanes], series[128:256, lanes]
            cosine, sine = digit_ref[2 * quad + k, 0], digit_ref[2 * quad + k, 1]
            re, im = re * cosine - im * sine, re * sine + im * cosine
            cosine, sine = near_ref[0], near_ref[1]
            work_ref[quad, 0:128, lanes] = re * cosine - im * sine
            work_ref[quad, 128:256, lanes] = re * sine + im * cosine

    def collect(step, carry):
        values = []
        for pair in range(8):
            lanes = slice(128 * (pair % 2), 128 * (pair % 2) + 128)
            rows = tile_rows(8 * step), tile_rows(128 + 8 * step)
            values.append((work_ref[pair // 2, rows[0], lanes], work_ref[pair // 2, rows[1], lanes]))
        for k, (re, im) in enumerate(butterfly(values, 1)):
            last_ref[k, tile_rows(8 * step), 0:128] = re
            last_ref[k, tile_rows(8 * step), 128:256] = im
        return carry

    lax.fori_loop(0, 16, collect, 0, unroll=4)
    for copy in waits[1]:
        copy.wait()
    for k in range(8):
        high, low = halves(last_ref[k])
        mixed = dot(high, mix_ref[0, k]) + dot(low, mix_ref[0, k]) + dot(high, mix_ref[1, k])
        for quarter in range(4):
            rows = slice(32 * quarter, 32 * quarter + 32)
            out_ref[4 * k + quarter, base:base + 32, :] = mixed[rows, 0:128]
            out_ref[4 * k + quarter, base + 32:base + 64, :] = mixed[rows, 128:256]


def filter_first(member_ref, *refs):
    pieces, mix_hbm, tables, norm_ref = refs[:10], refs[10], refs[11:16], refs[16]
    out_ref, work_ref, last_ref, mix_ref, held_ref, sems = refs[17:]
    side, core = member_ref[0], member_ref[1]
    pairs = []
    for at, piece in enumerate(pieces):
        step, first = ((0, 0), (3, 0), (1, 0), (2, 0), (2, 16))[at % 5]
        slot = 2 * lax.rem(side + step, 4) + (core if at < 5 else 1 - core)
        pairs.append((piece, held_ref.at[slot, pl.ds(first, piece.shape[0])]))
    copies = fetch(pairs + [(mix_hbm, mix_ref)], sems)
    for rank in range(RANKS):
        out_ref[rank, 64:72, :] = norm_ref[...]
    for copy in copies[:10]:
        copy.wait()
    bank_ref, near_ref, table_ref, digit_ref, fold_ref = tables
    filter_detector(
        lambda member, rank: held_ref[member, rank],
        bank_ref, near_ref, mix_ref, table_ref, digit_ref, fold_ref, out_ref, 0, work_ref, last_ref, ((), copies[10:]),
    )


def filter_rest(in_hbm, bank_hbm, near_hbm, mix_hbm, table_hbm, digit_hbm, fold_hbm, out_ref, *scratch):
    work_ref, last_ref, bank_ref, near_ref, mix_ref, table_ref, digit_ref, fold_ref, held_ref, sems = scratch
    pairs = [(in_hbm.at[:, :, 8 * at:8 * at + 8, :], held_ref.at[at]) for at in range(2)]
    pairs = [pairs[0], (fold_hbm, fold_ref), (digit_hbm, digit_ref), (table_hbm, table_ref), (bank_hbm, bank_ref)] + [
        (near_hbm, near_ref), (mix_hbm, mix_ref), pairs[1]
    ]
    copies = fetch(pairs, sems)
    for copy in copies[:3]:
        copy.wait()
    for at in range(2):
        filter_detector(
            lambda member, rank, at=at: held_ref[at, member, rank],
            bank_ref, near_ref, mix_ref, table_ref, digit_ref, fold_ref, out_ref, 64 * at, work_ref, last_ref,
            ((), ()) if at else (copies[3:6], copies[6:8]),
        )


def detector_power(in_ref, base, twiddle_ref, wide_ref, work_ref):
    def step_fn(step, carry):
        values = [
            (in_ref[r, tile_rows(base + 8 * step), :], in_ref[r, tile_rows(base + 32 + 8 * step), :])
            for r in range(RANKS)
        ]
        for digit, (re, im) in enumerate(butterfly(values, 1)):
            cosine, sine = twiddle_ref[0, digit:digit + 1, :], twiddle_ref[1, digit:digit + 1, :]
            at = 16 * (digit // 16) + 4 * (digit % 4) + digit // 4 % 4
            rows = tile_rows(32 * at + 8 * step)
            work_ref[rows, 0:128] = re * cosine - im * sine
            work_ref[rows, 128:256] = im * cosine + re * sine
        return carry

    lax.fori_loop(0, 4, step_fn, 0, unroll=2)

    def power_of(quad):
        high, low = halves(work_ref[pl.ds(pl.multiple_of(128 * quad, 128), 128), :])
        full = dot(high, wide_ref[0]) + dot(low, wide_ref[0]) + dot(high, wide_ref[1])
        re, im = full[:, 0:128], full[:, 128:256]
        return re * re + im * im

    return power_of


def start_power(in_ref, twiddle_ref, wide_ref, out_ref, work_ref):
    total = jnp.zeros((8, 128), F32)
    for rank in range(RANKS):
        total = total + in_ref[rank, 64:72, :]
    out_ref[1024:1032, :] = total
    out_ref[1032:1096, :] = twiddle_ref[...].reshape(64, 128)
    power_of = detector_power(in_ref, 0, twiddle_ref, wide_ref, work_ref)

    def step_fn(quad, carry):
        out_ref[pl.ds(pl.multiple_of(128 * quad, 128), 128), :] = power_of(quad)
        return carry

    lax.fori_loop(0, 8, step_fn, 0)


def finish_power(in_ref, wide_ref, sum_ref, out_ref, one_ref, two_ref):
    twiddle_ref = sum_ref.at[1032:1096].reshape(2, 32, 128)
    first = detector_power(in_ref, 0, twiddle_ref, wide_ref, one_ref)
    second = detector_power(in_ref, 64, twiddle_ref, wide_ref, two_ref)
    scale = 1.0 / (FULL * (jnp.sum(sum_ref[1024:1032, :]) + EPSILON))
    for quad in range(8):
        rows = slice(128 * quad, 128 * quad + 128)
        turned = ((first(quad) + second(quad) + sum_ref[rows, :]) * scale).T
        for g in range(8):
            start = 32 * (quad // 4) + 4 * (quad % 4) + 16 * (g // 4) + g % 4
            out_ref[pl.ds(start, 16, stride=64), :] = turned[16 * g:16 * g + 16, :]


def best_template(*refs):
    refs[4][...] = jnp.maximum(jnp.maximum(refs[0][...], refs[1][...]), jnp.maximum(refs[2][...], refs[3][...]))


def merge_templates(side_ref, *refs):
    one_ref, two_ref, out_ref = refs[4:]
    for block in range(8):
        rows = slice(32 * block, 32 * block + 32)
        best = jnp.maximum(one_ref[rows, :], two_ref[rows, :])
        for step in range(4):
            t = lax.rem(side_ref[0] + (4 - step), 4)
            out_ref[4 * block + t, 0:32, :] = refs[step][rows, :]
            out_ref[4 * block + t, 32:64, :] = best


def place_samples(in_ref, out_ref, best_ref):
    for k in range(8):
        for first, target in ((0, out_ref), (32, best_ref)):
            parts = [in_ref[4 * k + quarter, first:first + 32, :] for quarter in range(4)]
            for u in range(4):
                joined = jnp.concatenate([p[:, 32 * u:32 * u + 32] for p in parts], axis=1)
                for h in range(2):
                    target[pl.ds(256 * u + 8 * h + k, 16, stride=16), :] = joined[16 * h:16 * h + 16]


def shape(*dims):
    return jax.ShapeDtypeStruct(dims, F32)


def call(kernel, out, specs, scratch=(), limit=VMEM_LIMIT, **kwargs):
    many = isinstance(out, (tuple, list))
    whole = pl.BlockSpec(memory_space=pltpu.VMEM)
    return pl.pallas_call(
        kernel,
        out_shape=out,
        in_specs=specs,
        out_specs=[whole] * len(out) if many else whole,
        scratch_shapes=list(scratch),
        compiler_params=pltpu.CompilerParams(vmem_limit_bytes=limit),
        **kwargs,
    )


def cost(us):
    return pl.CostEstimate(flops=int(us * 1e9), bytes_accessed=int(us * 1e6), transcendentals=0)


TIME = ("zp", "zl", "x")
BINS = ("zl", "x", "y")
ACROSS = [(0, 1), (1, 0)]


def forward(value, axis, step):
    return lax.ppermute(value, axis, [(i, (i + step) % 4) for i in range(4)]) if step else value


def gather_pieces(value, ready):
    half = value.shape[0] // 2
    back, ahead = forward(value, "zp", 1), forward(value, "zp", 3)
    own = [value, back, ahead, forward(back[:half], "zp", 1), forward(ahead[half:], "zp", 3)]
    own, ready = lax.optimization_barrier((own, ready))
    return own + [lax.ppermute(one, "core", ACROSS) for one in own], ready


def spread_templates(masked, y):
    pieces = [lax.dynamic_index_in_dim(masked, y, 0, False)]
    for step in (1, 2, 3):
        pieces.append(forward(lax.dynamic_index_in_dim(masked, (y + step) % 4, 0, False), "y", step))
    return jnp.stack(pieces)


def move_templates(pieces, y, side, step):
    return forward(lax.dynamic_index_in_dim(pieces, (y - side - step) % 4, 0, False), "zp", step)


def local(strain, templates, pattern, cutoff):
    side, low, x, y, core = (lax.axis_index(n).astype(jnp.int32) for n in ("zp", "zl", "x", "y", "core"))
    me, group, place = 8 * side + 4 * low + x, 2 * y + core, 16 * low + 4 * x + y
    vmem = pl.BlockSpec(memory_space=pltpu.VMEM)
    smem = pl.BlockSpec(memory_space=pltpu.SMEM)
    anywhere = pl.BlockSpec(memory_space=pl.ANY)

    samples = strain.reshape(2, 3, 64, 16, 128).transpose(1, 2, 3, 0, 4).reshape(192, 32, 128)
    columns = pl.pallas_call(
        lambda group_ref, strain_ref, out_ref: gather_columns(group_ref, strain_ref.reshape(1536, 128), out_ref),
        out_shape=shape(RANKS, 24, 128),
        grid_spec=pltpu.PrefetchScalarGridSpec(
            num_scalar_prefetch=1,
            grid=(1,),
            in_specs=[pl.BlockSpec((192, 8, 128), lambda i, at: (0, at[0] // 2, 0))],
            out_specs=pl.BlockSpec((RANKS, 24, 128), lambda i, at: (0, 0, 0)),
        ),
        compiler_params=pltpu.CompilerParams(vmem_limit_bytes=58 * 1024 * 1024),
        cost_estimate=cost(3),
    )(group.reshape(1), samples)
    columns, templates = lax.optimization_barrier((columns, templates))
    columns = lax.all_to_all(columns, TIME, 0, 0, tiled=True)

    block_index = jnp.arange(pattern.shape[1], dtype=jnp.int32)
    active = pattern.astype(F32) * (block_index[None, :] < cutoff[:, None]).astype(F32)
    weight = jnp.repeat(active, SIDE // pattern.shape[1], axis=1)
    masked = jnp.swapaxes(templates.reshape(2, 4, 16, SIDE), 0, 1) * weight
    pieces = spread_templates(masked, y)
    pieces, group, me, place = lax.optimization_barrier((pieces, group, me, place))
    moved = [move_templates(pieces, y, side, step) for step in (0, 1, 2, 3)]

    row = jnp.arange(256, dtype=jnp.int32)[:, None]
    lane = jnp.arange(128, dtype=jnp.int32)[None, :]
    first_phase = phases((256 * group + 8 * me + row % 8) * (row // 8 + 32 * (lane % 64)), -1.0)
    fixed = [jnp.asarray(t) for t in (row_twiddle(), first_table(2), first_table(1))]
    columns, first_phase, fixed = lax.optimization_barrier((columns, first_phase, fixed))

    def first_bins(columns, first_phase, *fixed):
        rows = call(
            first_section,
            shape(RANKS * 24, 128),
            [vmem] * 5,
            [pltpu.VMEM((256, 256), F32), pltpu.VMEM((256, 128), F32), pltpu.VMEM((3, 256, 128), F32)],
            cost_estimate=cost(4),
        )(columns, *fixed, first_phase)
        return lax.all_to_all(rows.reshape(RANKS, 24, 128), BINS, 0, 0, tiled=True)

    rows = lax.cond(place >= 0, first_bins, lambda columns, *rest: columns, columns, first_phase, *fixed)
    rows, moved, place = lax.optimization_barrier((rows, moved, place))
    near = phases(jnp.arange(128, dtype=jnp.int32)[:, None] * (512 * (lane // 16 % 4) + 16 * place + lane % 16), 1.0)
    mix = mixing_tables(place)
    bank, norm = call(
        prepare_templates,
        (shape(2, SIDE, 128), shape(8, 128)),
        [smem] + [anywhere] * 4,
        [pltpu.VMEM((4, 2, 16, SIDE), F32), pltpu.SemaphoreType.DMA((4,))],
        cost_estimate=cost(4),
    )(side.reshape(1), *moved)

    tables = [jnp.asarray(t) for t in (column_table(), digit_twiddle(), fold_twiddle())]
    others, early = lax.optimization_barrier((rows[:, 0:16, :], rows[:, 16:24, :]))
    others = lax.all_gather(others, ("zp", "core"), axis=0)
    pieces, (bank, near, mix) = gather_pieces(early, (bank, near, mix))
    work = [pltpu.VMEM((4, 256, 256), F32), pltpu.VMEM((8, 128, 256), F32)]
    mixing = pltpu.VMEM((2, 8, 256, 256), BF16)
    first = call(
        filter_first,
        shape(RANKS, 72, 128),
        [smem] + [anywhere] * 11 + [vmem] * 6,
        work + [mixing, pltpu.VMEM((GROUPS, RANKS, 8, 128), F32), pltpu.SemaphoreType.DMA((11,))],
        cost_estimate=cost(8),
    )(jnp.stack((side, core)), *pieces, mix, bank, near, *tables, norm)
    first = lax.all_to_all(first, BINS, 0, 0, tiled=True)
    second = call(
        filter_rest,
        shape(RANKS, 128, 128),
        [anywhere] * 7,
        work
        + [
            pltpu.VMEM((2, SIDE, 128), F32),
            pltpu.VMEM((2, 128, 128), F32),
            mixing,
            pltpu.VMEM((2, 2, 256, 256), BF16),
            pltpu.VMEM((8, 2, 128, 128), F32),
            pltpu.VMEM((8, 2, 128), F32),
            pltpu.VMEM((2, GROUPS, RANKS, 8, 128), F32),
            pltpu.SemaphoreType.DMA((8,)),
        ],
        limit=58 * 1024 * 1024,
        cost_estimate=cost(12),
    )(others, bank, near, mix, *tables)
    second = lax.all_to_all(second, BINS, 0, 0, tiled=True)

    twiddle, wide = jnp.asarray(inner_twiddle()), jnp.asarray(last_table())
    work = pltpu.VMEM((1024, 256), F32)
    total = call(start_power, shape(1096, 128), [vmem] * 3, [work], cost_estimate=cost(3))(first, twiddle, wide)
    power = call(finish_power, shape(1024, 128), [vmem] * 3, [work] * 2, cost_estimate=cost(6))(second, wide, total)
    power = power.reshape(4, 256, 128)
    power = [forward(lax.dynamic_index_in_dim(power, (side + step) % 4, 0, False), "zp", step) for step in range(4)]
    best = call(best_template, shape(256, 128), [vmem] * 4, cost_estimate=cost(1))(*power)
    other = lax.ppermute(best, "core", ACROSS)
    power = call(merge_templates, shape(RANKS, 64, 128), [smem] + [vmem] * 6, cost_estimate=cost(2))(
        side.reshape(1), *power, best, other
    )
    power = lax.all_to_all(power, BINS, 0, 0, tiled=True)
    snr, peak = call(place_samples, (shape(1024, 128), shape(1024, 128)), [vmem], cost_estimate=cost(2))(power)
    return snr.reshape(1, 64 * SIDE), peak.reshape(64 * SIDE)


def solution(mesh):
    mesh = jax.sharding.Mesh(mesh.devices.reshape(4, 2, 4, 4, 2), ("zp", "zl", "x", "y", "core"))
    group = ("y", "core")
    in_specs = (P(None, None, TIME), P(None, group, TIME, None), P(group, None), P(group))
    out_specs = (P(group, TIME), P(TIME))
    return jax.shard_map(local, mesh=mesh, in_specs=in_specs, out_specs=out_specs, check_vma=False)
```

```python
import functools
import math

import jax
import jax.numpy as jnp
import numpy as np
from jax import lax
from jax.experimental import pallas as pl
from jax.experimental.pallas import tpu as pltpu
from jax.sharding import PartitionSpec as P

EPSILON = 1e-06
SIDE = 2048
FULL = SIDE * SIDE
DETECTORS = 3
RANKS = 32
GROUPS = 8
F32 = jnp.float32
BF16 = jnp.bfloat16
VMEM_LIMIT = 24 * 1024 * 1024


def split_table(table):
    high = table.astype(np.float32).astype(jnp.bfloat16)
    low = (table - high.astype(np.float64)).astype(np.float32).astype(jnp.bfloat16)
    return np.stack((high, low))


def first_table(copies):
    theta = 2.0 * np.pi * np.outer(np.arange(64), np.arange(64)) / 64.0
    eye = np.eye(copies)
    cosine, sine = np.kron(eye, np.cos(theta)), np.kron(eye, np.sin(theta))
    return split_table(np.block([[cosine, -sine], [sine, cosine]]))


def last_table():
    theta = 2.0 * np.pi * np.outer(np.arange(16), np.arange(16)) / 16.0
    eye = np.eye(8)
    cosine, sine = np.kron(eye, np.cos(theta)), np.kron(eye, np.sin(theta))
    return split_table(np.block([[cosine, sine], [-sine, cosine]]))


def column_table():
    theta = 2.0 * np.pi * np.outer(np.arange(128), np.arange(128)) / 128.0
    cosine, sine = np.cos(theta), np.sin(theta)
    whole = np.block([[cosine, sine], [-sine, cosine]])
    return np.stack((split_table(whole), split_table(whole.T)))


def digit_twiddle():
    digit = 2 * np.arange(8)[:, None, None] + (np.arange(128) // 64)[None, None, :]
    theta = 2.0 * np.pi * (np.arange(128)[None, :, None] * digit) / SIDE
    return np.stack((np.cos(theta), np.sin(theta)), axis=1).astype(np.float32)


def fold_twiddle():
    theta = 2.0 * np.pi * np.outer(np.arange(8), np.arange(128) // 64) / 16.0
    return np.stack((np.cos(theta), -np.sin(theta)), axis=1).astype(np.float32)


def row_twiddle():
    theta = 2.0 * np.pi * np.outer(np.arange(32), np.arange(128) % 64) / SIDE
    return np.stack((np.cos(theta), np.sin(theta))).astype(np.float32)


def inner_twiddle():
    theta = 2.0 * np.pi * np.outer(np.arange(32), np.arange(128) % 16) / 512.0
    return np.stack((np.cos(theta), np.sin(theta))).astype(np.float32)


def phases(turns, orient):
    angle = (turns % FULL).astype(F32) * (orient * 2.0 * math.pi / FULL)
    return jnp.stack((jnp.cos(angle), jnp.sin(angle)))


def mixing_tables(place):
    k = jnp.arange(8, dtype=jnp.int32)[:, None, None]
    into = jnp.arange(128, dtype=jnp.int32)[None, :, None]
    out = jnp.arange(128, dtype=jnp.int32)[None, None, :]
    block, w = k + 8 * (out // 64), out // 16 % 4
    e, a, i = into // 64, into // 16 % 4, into % 16
    turns = e * block * (FULL // 16) + 128 * block * (512 * a + 16 * place + i)
    turns = turns % FULL + a * w * (FULL // 4) + (16 * place + i) * w * SIDE
    cosine, sine = phases(turns, 1.0) * (i == out % 16).astype(F32)
    whole = jnp.concatenate(
        (jnp.concatenate((cosine, sine), axis=2), jnp.concatenate((-sine, cosine), axis=2)), axis=1
    )
    high = lax.reduce_precision(whole, 8, 7)
    return jnp.stack((high.astype(BF16), (whole - high).astype(BF16)))


def times_unit(value, numer, denom, orient):
    re, im = value
    numer = numer % denom
    if numer == 0:
        return value
    if 8 * numer % denom == 0:
        eighth = 8 * numer // denom
        if eighth == 4:
            return -re, -im
        if eighth in (2, 6):
            return (-im, re) if (eighth == 2) == (orient > 0) else (im, -re)
    cosine = math.cos(2.0 * math.pi * numer / denom)
    sine = orient * math.sin(2.0 * math.pi * numer / denom)
    return re * cosine - im * sine, re * sine + im * cosine


def butterfly(values, orient):
    count = len(values)
    if count == 1:
        return values
    if count == 2:
        (ar, ai), (br, bi) = values
        return [(ar + br, ai + bi), (ar - br, ai - bi)]
    if count == 4:
        (ar, ai), (br, bi), (cr, ci), (dr, di) = values
        sr, si, tr, ti = ar + cr, ai + ci, ar - cr, ai - ci
        ur, ui, vr, vi = br + dr, bi + di, br - dr, bi - di
        if orient > 0:
            return [(sr + ur, si + ui), (tr - vi, ti + vr), (sr - ur, si - ui), (tr + vi, ti - vr)]
        return [(sr + ur, si + ui), (tr + vi, ti - vr), (sr - ur, si - ui), (tr - vi, ti + vr)]
    radix = 4 if count % 4 == 0 else 2
    inner = count // radix
    parts = [butterfly(values[s::radix], orient) for s in range(radix)]
    out = [None] * count
    for k in range(inner):
        joined = butterfly([times_unit(parts[s][k], s * k, count, orient) for s in range(radix)], orient)
        for part in range(radix):
            out[k + inner * part] = joined[part]
    return out


def halves(value):
    high = value.astype(BF16)
    return high, (value - high.astype(F32)).astype(BF16)


def dot(a, b, contract=((1,), (0,))):
    return lax.dot_general(a, b, (contract, ((), ())), preferred_element_type=F32)


def low_lanes(shape):
    return lax.broadcasted_iota(jnp.int32, shape, 1) < 64


def swap(value):
    return pltpu.roll(value, 64, 1)


def fetch(pairs, sems):
    copies = [pltpu.make_async_copy(source, target, sems.at[at]) for at, (source, target) in enumerate(pairs)]
    for copy in copies:
        copy.start()
    return copies


def tile_rows(start):
    return pl.ds(pl.multiple_of(start, 8), 8)


def gather_columns(group_ref, strain_ref, out_ref):
    first = 4 * lax.rem(group_ref[0], 2)

    def piece(detector, tile, part):
        return strain_ref[pl.ds(512 * detector + first + 2 * tile + part, 64, stride=8), :]

    for tile in range(2):
        for at, (one, two) in enumerate((((0, 0), (1, 0)), ((0, 1), (1, 1)), ((2, 0), (2, 1)))):
            joined = jnp.concatenate((piece(one[0], tile, one[1]), piece(two[0], tile, two[1])), axis=0)
            out_ref[16 * tile:16 * tile + 16, 8 * at:8 * at + 8, :] = joined.T.reshape(16, 8, 128)


def prepare_templates(side_ref, *refs):
    pieces, (out_ref, norm_ref, held_ref, sems) = refs[:4], refs[4:]
    copies = []
    for at, piece in enumerate(pieces):
        copy = pltpu.make_async_copy(piece, held_ref.at[lax.rem(side_ref[0] + (4 - at), 4)], sems.at[at])
        copy.start()
        copies.append(copy)
    for copy in copies:
        copy.wait()
    total = jnp.zeros((64, 128), F32)
    for chunk in range(16):
        lanes = slice(128 * chunk, 128 * chunk + 128)
        for part in range(2):
            value = jnp.concatenate([held_ref[a, part, :, lanes] for a in range(4)], axis=0)
            total = total + value * value
            out_ref[part, lanes, :] = jnp.concatenate((value, pltpu.roll(value, 127, 1)), axis=0).T
    norm_ref[...] = jnp.sum(total.reshape(8, 8, 128), axis=0)


def first_section(in_ref, twiddle_ref, wide_ref, narrow_ref, phase_ref, out_ref, pair_ref, single_ref, turn_ref):
    lower = low_lanes((8, 128))
    for at in range(2):
        values = []
        for rank in range(RANKS):
            if at == 0:
                values.append((in_ref[rank, 0:8, :], in_ref[rank, 8:16, :]))
            else:
                one = in_ref[rank, 16:24, :]
                values.append((one, swap(one)))
        for digit, (re, im) in enumerate(butterfly(values, -1)):
            cosine, sine = twiddle_ref[0, digit:digit + 1, :], twiddle_ref[1, digit:digit + 1, :]
            re, im = re * cosine + im * sine, im * cosine - re * sine
            rows = slice(8 * digit, 8 * digit + 8)
            if at == 0:
                pair_ref[rows, 0:128] = re
                pair_ref[rows, 128:256] = im
            else:
                single_ref[rows, :] = jnp.where(lower, re, swap(im))
    high, low = halves(pair_ref[...])
    pair = dot(high, wide_ref[0]) + dot(low, wide_ref[0]) + dot(high, wide_ref[1])
    high, low = halves(single_ref[...])
    single = dot(high, narrow_ref[0]) + dot(low, narrow_ref[0]) + dot(high, narrow_ref[1])
    cosine, sine = phase_ref[0], phase_ref[1]
    re, im = pair[:, 0:128], pair[:, 128:256]
    turn_ref[0] = re * cosine - im * sine
    turn_ref[1] = im * cosine + re * sine
    turn_ref[2] = single * cosine + swap(single) * jnp.where(low_lanes((256, 128)), -sine, sine)
    for at in range(DETECTORS):
        for quad in range(2):
            blocks = []
            for part in range(2):
                source, start = (part, 64 * at) if at < 2 else (2, 64 * part)
                cols = [turn_ref[source, pl.ds(4 * quad + u, 32, stride=8), :] for u in range(4)]
                for a in range(4):
                    lanes = slice(start + 16 * a, start + 16 * a + 16)
                    blocks.append(jnp.concatenate([c[16 * h:16 * h + 16, lanes] for c in cols for h in range(2)], axis=1))
            turned = jnp.concatenate(blocks, axis=0).T
            for u in range(4):
                for h in range(2):
                    rows = pl.ds(24 * h + 8 * at + 4 * quad + u, 16, stride=48)
                    out_ref[rows, :] = turned[32 * u + 16 * h:32 * u + 16 * h + 16, :]


def slot_of(a, low):
    return 4 * (a % 2) + 2 * (low // 8) + a // 2 % 2, 16 * (low // 4 % 2) + 4 * (low % 4) + a // 4


def filter_detector(
    load, template_ref, near_ref, mix_ref, table_ref, digit_ref, fold_ref, out_ref, base, work_ref, last_ref, waits
):
    lower = low_lanes((8, 128))

    def spread(low, carry):
        values = []
        for a in range(8):
            one = load(*slot_of(a, low))
            two = load(*slot_of(a + 8, low))
            add, sub = one + two, one - two
            re, im = jnp.where(lower, add, swap(sub)), jnp.where(lower, swap(add), sub)
            cosine, sine = fold_ref[a, 0:1, :], fold_ref[a, 1:2, :]
            values.append((re * cosine - im * sine, re * sine + im * cosine) if a else (re, im))
        for pair, (re, im) in enumerate(butterfly(values, -1)):
            cosine, sine = digit_ref[pair, 0, tile_rows(8 * low), :], digit_ref[pair, 1, tile_rows(8 * low), :]
            lanes = slice(128 * (pair % 2), 128 * (pair % 2) + 128)
            work_ref[pair // 2, tile_rows(8 * low), lanes] = re * cosine + im * sine
            work_ref[pair // 2, tile_rows(128 + 8 * low), lanes] = im * cosine - re * sine
        return carry

    lax.fori_loop(0, 16, spread, 0, unroll=8)
    for copy in waits[0]:
        copy.wait()

    for quad in range(4):
        high, low = halves(work_ref[quad])
        spectrum = dot(table_ref[0, 0], high) + dot(table_ref[0, 0], low) + dot(table_ref[0, 1], high)
        s_re, s_im = spectrum[0:128], spectrum[128:256]
        rows = [pl.ds(4 * quad + 2 * k, 128, stride=16) for k in range(2)]
        h_re = jnp.concatenate([template_ref[0, r, :] for r in rows], axis=1)
        h_im = jnp.concatenate([template_ref[1, r, :] for r in rows], axis=1)
        product = jnp.concatenate((s_re * h_re + s_im * h_im, s_im * h_re - s_re * h_im), axis=0)
        high, low = halves(product)
        series = dot(table_ref[1, 0], high) + dot(table_ref[1, 0], low) + dot(table_ref[1, 1], high)
        for k in range(2):
            lanes = slice(128 * k, 128 * k + 128)
            re, im = series[0:128, lanes], series[128:256, lanes]
            cosine, sine = digit_ref[2 * quad + k, 0], digit_ref[2 * quad + k, 1]
            re, im = re * cosine - im * sine, re * sine + im * cosine
            cosine, sine = near_ref[0], near_ref[1]
            work_ref[quad, 0:128, lanes] = re * cosine - im * sine
            work_ref[quad, 128:256, lanes] = re * sine + im * cosine

    def collect(step, carry):
        values = []
        for pair in range(8):
            lanes = slice(128 * (pair % 2), 128 * (pair % 2) + 128)
            rows = tile_rows(8 * step), tile_rows(128 + 8 * step)
            values.append((work_ref[pair // 2, rows[0], lanes], work_ref[pair // 2, rows[1], lanes]))
        for k, (re, im) in enumerate(butterfly(values, 1)):
            last_ref[k, tile_rows(8 * step), 0:128] = re
            last_ref[k, tile_rows(8 * step), 128:256] = im
        return carry

    lax.fori_loop(0, 16, collect, 0, unroll=8)
    for copy in waits[1]:
        copy.wait()
    for k in range(8):
        high, low = halves(last_ref[k])
        mixed = dot(high, mix_ref[0, k]) + dot(low, mix_ref[0, k]) + dot(high, mix_ref[1, k])
        for quarter in range(4):
            rows = slice(32 * quarter, 32 * quarter + 32)
            out_ref[4 * k + quarter, base:base + 32, :] = mixed[rows, 0:128]
            out_ref[4 * k + quarter, base + 32:base + 64, :] = mixed[rows, 128:256]


def filter_first(member_ref, *refs):
    pieces, mix_hbm, tables, norm_ref = refs[:10], refs[10], refs[11:16], refs[16]
    out_ref, work_ref, last_ref, mix_ref, held_ref, sems = refs[17:]
    side, core = member_ref[0], member_ref[1]
    pairs = []
    for at, piece in enumerate(pieces):
        step, first = ((0, 0), (3, 0), (1, 0), (2, 0), (2, 16))[at % 5]
        slot = 2 * lax.rem(side + step, 4) + (core if at < 5 else 1 - core)
        pairs.append((piece, held_ref.at[slot, pl.ds(first, piece.shape[0])]))
    copies = fetch(pairs + [(mix_hbm, mix_ref)], sems)
    for rank in range(RANKS):
        out_ref[rank, 64:72, :] = norm_ref[...]
    for copy in copies[:10]:
        copy.wait()
    bank_ref, near_ref, table_ref, digit_ref, fold_ref = tables
    filter_detector(
        lambda member, rank: held_ref[member, rank],
        bank_ref, near_ref, mix_ref, table_ref, digit_ref, fold_ref, out_ref, 0, work_ref, last_ref, ((), copies[10:]),
    )


def filter_rest(in_hbm, bank_hbm, near_hbm, mix_hbm, table_hbm, digit_hbm, fold_hbm, out_ref, *scratch):
    work_ref, last_ref, bank_ref, near_ref, mix_ref, table_ref, digit_ref, fold_ref, held_ref, sems = scratch
    pairs = [(in_hbm.at[:, :, 8 * at:8 * at + 8, :], held_ref.at[at]) for at in range(2)]
    pairs = [pairs[0], (fold_hbm, fold_ref), (digit_hbm, digit_ref), (table_hbm, table_ref), (bank_hbm, bank_ref)] + [
        (near_hbm, near_ref), (mix_hbm, mix_ref), pairs[1]
    ]
    copies = fetch(pairs, sems)
    for copy in copies[:3]:
        copy.wait()
    for at in range(2):
        filter_detector(
            lambda member, rank, at=at: held_ref[at, member, rank],
            bank_ref, near_ref, mix_ref, table_ref, digit_ref, fold_ref, out_ref, 64 * at, work_ref, last_ref,
            ((), ()) if at else (copies[3:6], copies[6:8]),
        )


def detector_power(in_ref, base, twiddle_ref, wide_ref, work_ref):
    def step_fn(step, carry):
        values = [
            (in_ref[r, tile_rows(base + 8 * step), :], in_ref[r, tile_rows(base + 32 + 8 * step), :])
            for r in range(RANKS)
        ]
        for digit, (re, im) in enumerate(butterfly(values, 1)):
            cosine, sine = twiddle_ref[0, digit:digit + 1, :], twiddle_ref[1, digit:digit + 1, :]
            at = 16 * (digit // 16) + 4 * (digit % 4) + digit // 4 % 4
            rows = tile_rows(32 * at + 8 * step)
            work_ref[rows, 0:128] = re * cosine - im * sine
            work_ref[rows, 128:256] = im * cosine + re * sine
        return carry

    lax.fori_loop(0, 4, step_fn, 0, unroll=2)

    def power_of(quad):
        high, low = halves(work_ref[pl.ds(pl.multiple_of(128 * quad, 128), 128), :])
        full = dot(high, wide_ref[0]) + dot(low, wide_ref[0]) + dot(high, wide_ref[1])
        re, im = full[:, 0:128], full[:, 128:256]
        return re * re + im * im

    return power_of


def start_power(in_ref, twiddle_ref, wide_ref, out_ref, work_ref):
    total = jnp.zeros((8, 128), F32)
    for rank in range(RANKS):
        total = total + in_ref[rank, 64:72, :]
    out_ref[1024:1032, :] = total
    out_ref[1032:1096, :] = twiddle_ref[...].reshape(64, 128)
    power_of = detector_power(in_ref, 0, twiddle_ref, wide_ref, work_ref)

    def step_fn(quad, carry):
        out_ref[pl.ds(pl.multiple_of(128 * quad, 128), 128), :] = power_of(quad)
        return carry

    lax.fori_loop(0, 8, step_fn, 0)


def finish_power(in_ref, wide_ref, sum_ref, out_ref, one_ref, two_ref):
    twiddle_ref = sum_ref.at[1032:1096].reshape(2, 32, 128)
    first = detector_power(in_ref, 0, twiddle_ref, wide_ref, one_ref)
    second = detector_power(in_ref, 64, twiddle_ref, wide_ref, two_ref)
    scale = 1.0 / (FULL * (jnp.sum(sum_ref[1024:1032, :]) + EPSILON))
    for quad in range(8):
        rows = slice(128 * quad, 128 * quad + 128)
        turned = ((first(quad) + second(quad) + sum_ref[rows, :]) * scale).T
        for g in range(8):
            start = 32 * (quad // 4) + 4 * (quad % 4) + 16 * (g // 4) + g % 4
            out_ref[pl.ds(start, 16, stride=64), :] = turned[16 * g:16 * g + 16, :]


def best_template(*refs):
    refs[4][...] = jnp.maximum(jnp.maximum(refs[0][...], refs[1][...]), jnp.maximum(refs[2][...], refs[3][...]))


def merge_templates(side_ref, *refs):
    one_ref, two_ref, out_ref = refs[4:]
    for block in range(8):
        rows = slice(32 * block, 32 * block + 32)
        best = jnp.maximum(one_ref[rows, :], two_ref[rows, :])
        for step in range(4):
            t = lax.rem(side_ref[0] + (4 - step), 4)
            out_ref[4 * block + t, 0:32, :] = refs[step][rows, :]
            out_ref[4 * block + t, 32:64, :] = best


def place_samples(in_ref, out_ref, best_ref):
    for k in range(8):
        for first, target in ((0, out_ref), (32, best_ref)):
            parts = [in_ref[4 * k + quarter, first:first + 32, :] for quarter in range(4)]
            for u in range(4):
                joined = jnp.concatenate([p[:, 32 * u:32 * u + 32] for p in parts], axis=1)
                for h in range(2):
                    target[pl.ds(256 * u + 8 * h + k, 16, stride=16), :] = joined[16 * h:16 * h + 16]


def shape(*dims):
    return jax.ShapeDtypeStruct(dims, F32)


def call(kernel, out, specs, scratch=(), limit=VMEM_LIMIT, **kwargs):
    many = isinstance(out, (tuple, list))
    whole = pl.BlockSpec(memory_space=pltpu.VMEM)
    return pl.pallas_call(
        kernel,
        out_shape=out,
        in_specs=specs,
        out_specs=[whole] * len(out) if many else whole,
        scratch_shapes=list(scratch),
        compiler_params=pltpu.CompilerParams(vmem_limit_bytes=limit),
        **kwargs,
    )


def cost(us):
    return pl.CostEstimate(flops=int(us * 1e9), bytes_accessed=int(us * 1e6), transcendentals=0)


TIME = ("zp", "zl", "x")
BINS = ("zl", "x", "y")
ACROSS = [(0, 1), (1, 0)]


def forward(value, axis, step):
    return lax.ppermute(value, axis, [(i, (i + step) % 4) for i in range(4)]) if step else value


def gather_pieces(value, ready):
    half = value.shape[0] // 2
    back, ahead = forward(value, "zp", 1), forward(value, "zp", 3)
    own = [value, back, ahead, forward(back[:half], "zp", 1), forward(ahead[half:], "zp", 3)]
    own, ready = lax.optimization_barrier((own, ready))
    return own + [lax.ppermute(one, "core", ACROSS) for one in own], ready


def spread_templates(masked, y):
    pieces = [lax.dynamic_index_in_dim(masked, y, 0, False)]
    for step in (1, 2, 3):
        pieces.append(forward(lax.dynamic_index_in_dim(masked, (y + step) % 4, 0, False), "y", step))
    return jnp.stack(pieces)


def move_templates(pieces, y, side, step):
    return forward(lax.dynamic_index_in_dim(pieces, (y - side - step) % 4, 0, False), "zp", step)


def local(strain, templates, pattern, cutoff):
    side, low, x, y, core = (lax.axis_index(n).astype(jnp.int32) for n in ("zp", "zl", "x", "y", "core"))
    me, group, place = 8 * side + 4 * low + x, 2 * y + core, 16 * low + 4 * x + y
    vmem = pl.BlockSpec(memory_space=pltpu.VMEM)
    smem = pl.BlockSpec(memory_space=pltpu.SMEM)
    anywhere = pl.BlockSpec(memory_space=pl.ANY)

    samples = strain.reshape(2, 3, 64, 16, 128).transpose(1, 2, 3, 0, 4).reshape(192, 32, 128)
    columns = pl.pallas_call(
        lambda group_ref, strain_ref, out_ref: gather_columns(group_ref, strain_ref.reshape(1536, 128), out_ref),
        out_shape=shape(RANKS, 24, 128),
        grid_spec=pltpu.PrefetchScalarGridSpec(
            num_scalar_prefetch=1,
            grid=(1,),
            in_specs=[pl.BlockSpec((192, 8, 128), lambda i, at: (0, at[0] // 2, 0))],
            out_specs=pl.BlockSpec((RANKS, 24, 128), lambda i, at: (0, 0, 0)),
        ),
        compiler_params=pltpu.CompilerParams(vmem_limit_bytes=58 * 1024 * 1024),
        cost_estimate=cost(3),
    )(group.reshape(1), samples)
    columns, templates = lax.optimization_barrier((columns, templates))
    columns = lax.all_to_all(columns, TIME, 0, 0, tiled=True)

    block_index = jnp.arange(pattern.shape[1], dtype=jnp.int32)
    active = pattern.astype(F32) * (block_index[None, :] < cutoff[:, None]).astype(F32)
    weight = jnp.repeat(active, SIDE // pattern.shape[1], axis=1)
    masked = jnp.swapaxes(templates.reshape(2, 4, 16, SIDE), 0, 1) * weight
    pieces = spread_templates(masked, y)
    pieces, group, me, place = lax.optimization_barrier((pieces, group, me, place))
    moved = [move_templates(pieces, y, side, step) for step in (0, 1, 2, 3)]

    row = jnp.arange(256, dtype=jnp.int32)[:, None]
    lane = jnp.arange(128, dtype=jnp.int32)[None, :]
    first_phase = phases((256 * group + 8 * me + row % 8) * (row // 8 + 32 * (lane % 64)), -1.0)
    fixed = [jnp.asarray(t) for t in (row_twiddle(), first_table(2), first_table(1))]
    columns, first_phase, fixed = lax.optimization_barrier((columns, first_phase, fixed))

    def first_bins(columns, first_phase, *fixed):
        rows = call(
            first_section,
            shape(RANKS * 24, 128),
            [vmem] * 5,
            [pltpu.VMEM((256, 256), F32), pltpu.VMEM((256, 128), F32), pltpu.VMEM((3, 256, 128), F32)],
            cost_estimate=cost(4),
        )(columns, *fixed, first_phase)
        return lax.all_to_all(rows.reshape(RANKS, 24, 128), BINS, 0, 0, tiled=True)

    rows = lax.cond(place >= 0, first_bins, lambda columns, *rest: columns, columns, first_phase, *fixed)
    rows, moved, place = lax.optimization_barrier((rows, moved, place))
    near = phases(jnp.arange(128, dtype=jnp.int32)[:, None] * (512 * (lane // 16 % 4) + 16 * place + lane % 16), 1.0)
    mix = mixing_tables(place)
    bank, norm = call(
        prepare_templates,
        (shape(2, SIDE, 128), shape(8, 128)),
        [smem] + [anywhere] * 4,
        [pltpu.VMEM((4, 2, 16, SIDE), F32), pltpu.SemaphoreType.DMA((4,))],
        cost_estimate=cost(4),
    )(side.reshape(1), *moved)

    tables = [jnp.asarray(t) for t in (column_table(), digit_twiddle(), fold_twiddle())]
    others, early = lax.optimization_barrier((rows[:, 0:16, :], rows[:, 16:24, :]))
    others = lax.all_gather(others, ("zp", "core"), axis=0)
    pieces, (bank, near, mix) = gather_pieces(early, (bank, near, mix))
    work = [pltpu.VMEM((4, 256, 256), F32), pltpu.VMEM((8, 128, 256), F32)]
    mixing = pltpu.VMEM((2, 8, 256, 256), BF16)
    first = call(
        filter_first,
        shape(RANKS, 72, 128),
        [smem] + [anywhere] * 11 + [vmem] * 6,
        work + [mixing, pltpu.VMEM((GROUPS, RANKS, 8, 128), F32), pltpu.SemaphoreType.DMA((11,))],
        cost_estimate=cost(8),
    )(jnp.stack((side, core)), *pieces, mix, bank, near, *tables, norm)
    first = lax.all_to_all(first, BINS, 0, 0, tiled=True)
    second = call(
        filter_rest,
        shape(RANKS, 128, 128),
        [anywhere] * 7,
        work
        + [
            pltpu.VMEM((2, SIDE, 128), F32),
            pltpu.VMEM((2, 128, 128), F32),
            mixing,
            pltpu.VMEM((2, 2, 256, 256), BF16),
            pltpu.VMEM((8, 2, 128, 128), F32),
            pltpu.VMEM((8, 2, 128), F32),
            pltpu.VMEM((2, GROUPS, RANKS, 8, 128), F32),
            pltpu.SemaphoreType.DMA((8,)),
        ],
        limit=58 * 1024 * 1024,
        cost_estimate=cost(12),
    )(others, bank, near, mix, *tables)
    second = lax.all_to_all(second, BINS, 0, 0, tiled=True)

    twiddle, wide = jnp.asarray(inner_twiddle()), jnp.asarray(last_table())
    work = pltpu.VMEM((1024, 256), F32)
    total = call(start_power, shape(1096, 128), [vmem] * 3, [work], cost_estimate=cost(3))(first, twiddle, wide)
    power = call(finish_power, shape(1024, 128), [vmem] * 3, [work] * 2, cost_estimate=cost(6))(second, wide, total)
    power = power.reshape(4, 256, 128)
    power = [forward(lax.dynamic_index_in_dim(power, (side + step) % 4, 0, False), "zp", step) for step in range(4)]
    best = call(best_template, shape(256, 128), [vmem] * 4, cost_estimate=cost(1))(*power)
    other = lax.ppermute(best, "core", ACROSS)
    power = call(merge_templates, shape(RANKS, 64, 128), [smem] + [vmem] * 6, cost_estimate=cost(2))(
        side.reshape(1), *power, best, other
    )
    power = lax.all_to_all(power, BINS, 0, 0, tiled=True)
    snr, peak = call(place_samples, (shape(1024, 128), shape(1024, 128)), [vmem], cost_estimate=cost(2))(power)
    return snr.reshape(1, 64 * SIDE), peak.reshape(64 * SIDE)


def solution(mesh):
    mesh = jax.sharding.Mesh(mesh.devices.reshape(4, 2, 4, 4, 2), ("zp", "zl", "x", "y", "core"))
    group = ("y", "core")
    in_specs = (P(None, None, TIME), P(None, group, TIME, None), P(group, None), P(group))
    out_specs = (P(group, TIME), P(TIME))
    return jax.shard_map(local, mesh=mesh, in_specs=in_specs, out_specs=out_specs, check_vma=False)
```
